256 devices in a mesh: panel: 2 (over z_hi), lat: 8 (over y, core), lon: 16 (over x, z_lo).
Axes of the slice: x: 4, y: 4, z: 8 (z_hi: 2, z_lo: 4; z = z_hi * 4 + z_lo), core: 2. Of those that a mesh axis runs over, the one named last changes fastest.
Arguments:
- tracers: float32 [2, 2, 36, 512, 2048], P('panel', None, None, 'lat', 'lon'), may hold values from -6 to 6
- winds: float32 [2, 2, 36, 512, 2048], P('panel', None, None, 'lat', 'lon'), may hold values from -0.3 to 0.3
- mixing: float32 [2, 35, 512, 2048], P('panel', None, 'lat', 'lon'), may hold values from 0.05 to 5
- strip_source: int32 [2, 320], replicated, may hold values from 0 to 127, as said below
- strip_tile: int32 [2, 320], replicated, may hold values from 0 to 127
- weights: bfloat16 [2, 320, 32, 64], replicated, may hold values from -1.5 to 1.5
Outputs:
- tracers_out: float32 [2, 2, 36, 512, 2048], P('panel', None, None, 'lat', 'lon')
The draws below stay inside these ranges and needn't reach their ends.
Inputs may be any that keep to these rules, and one draw needn't show every extreme that they name: strip_source numbers a device of the other panel as its row of devices times (16) plus its column of devices. Strips 2m and 2m + 1 of a list have the same source device and lie on the same device; the pairs of strips that lie on one device come from distinct source devices. Over one panel's list, no device is named by more than 2 pairs of strips, and some device by exactly 2.
All inputs are finite; a program needn't handle non-finite values.
Results may differ from the reference program's by a relative error of at most 0.0003.
Values sent between devices are 32-bit elements; how exact they have to be, the bound alone decides.
A program may use at most 128 MiB of HBM per device.

```python
import math
import jax
import jax.numpy as jnp
from jax import lax

TRACERS = 2
LEVELS = 36
CLAT = 64
CLON = 128
STEPS = 2
STRIP = 32
TILE = 64
NLAT = 512
NLON = 2048
NSTRIP = 320
NTILE = 128
N_LAT = 8
N_LON = 16


def draw_strip_source(key, part):
    key = jax.random.fold_in(key, 11)
    device_count = N_LAT * N_LON
    across_count = CLON // 16
    down_count = CLAT // 16
    pair_count = (across_count + down_count) // 2
    device_ids = jnp.arange(device_count, dtype=jnp.int32)
    device_lat = device_ids // N_LON
    device_lon = device_ids % N_LON
    band_ok = (device_lat == 0) | (device_lat == N_LAT - 1)
    side_ok = (device_lon == 0) | (device_lon == N_LON - 1)
    pair_ids = jnp.arange(pair_count, dtype=jnp.int32)
    pair_valid = jnp.where(pair_ids[None, :] < across_count // 2, band_ok[:, None], side_ok[:, None])
    flat_valid = pair_valid.astype(jnp.int32).reshape(-1)
    order_index = jnp.cumsum(flat_valid) - flat_valid

    def one_panel(panel_number):
        panel_key = jax.random.fold_in(key, panel_number)
        remaining = 1 + jax.random.permutation(panel_key, device_count - 2).astype(jnp.int32)
        order = jnp.concatenate([jnp.array([device_count - 1, 0], jnp.int32), remaining])
        return jnp.take(order, order_index % device_count).reshape(device_count, pair_count)
    table = jax.vmap(one_panel)(jnp.arange(2, dtype=jnp.int32))
    across_band = N_LON * across_count
    down_band = N_LAT * down_count
    strip_ids = jnp.arange(2 * across_band + 2 * down_band, dtype=jnp.int32)
    in_north = strip_ids < across_band
    in_west = (strip_ids >= 2 * across_band) & (strip_ids < 2 * across_band + down_band)
    is_band = strip_ids < 2 * across_band
    band_offset = jnp.where(in_north, strip_ids, strip_ids - across_band)
    side_offset = jnp.where(in_west, strip_ids - 2 * across_band, strip_ids - 2 * across_band - down_band)
    band_dest = jnp.where(in_north, 0, N_LAT - 1) * N_LON + band_offset // across_count
    band_slot = band_offset % across_count
    side_dest = side_offset // down_count * N_LON + jnp.where(in_west, 0, N_LON - 1)
    side_slot = across_count + side_offset % down_count
    dest_device = jnp.where(is_band, band_dest, side_dest)
    dest_slot = jnp.where(is_band, band_slot, side_slot)
    return table[:, dest_device, dest_slot // 2]


def set_ends(values, stream_key, low, high):
    place = [jax.random.randint(jax.random.fold_in(stream_key, axis), (), 0, length) for axis, length in enumerate(values.shape)]
    main_axis = values.shape.index(max(values.shape))
    next_to = place[:main_axis] + [(place[main_axis] + 1) % values.shape[main_axis]] + place[main_axis + 1:]
    return values.at[tuple(place)].set(low).at[tuple(next_to)].set(high)


def block_levels(own_key, extent, split, smallest, top_value):
    def one(position, shards_of):
        draws = jax.random.uniform(jax.random.fold_in(jax.random.fold_in(own_key, 6), position), (shards_of,), jnp.float32, smallest / len(split), top_value / len(split))
        return jnp.repeat(jnp.exp(draws), extent[position] // shards_of).reshape((-1,) + (1,) * (len(extent) - position - 1))

    factor_of = one(*split[0])
    for cut in split[1:]:
        factor_of = factor_of * one(*cut)
    return factor_of


def centred(stream_key, extent, scale, bound, cuts=(), kind=jnp.bfloat16):
    loudness = block_levels(stream_key, extent, cuts, -0.22, 0.18) if cuts else 1.0
    result = jax.random.normal(stream_key, extent, jnp.float32) * scale * loudness
    return jnp.minimum(jnp.maximum(result, -bound), bound).astype(kind)


def setup_inputs(seed: int = 0) -> dict:
    seeds = jax.random.split(jax.random.key(seed), 7)
    tracers = centred(seeds[0], (2, TRACERS, LEVELS, NLAT, NLON), 1.0, 6.0, ((0, 2), (3, 8), (4, 16)), jnp.float32)
    winds = jnp.clip(jax.random.uniform(seeds[1], (2, 2, LEVELS, NLAT, NLON), jnp.float32, -0.3, 0.3) * block_levels(seeds[1], (2, 2, LEVELS, NLAT, NLON), ((0, 2), (3, 8), (4, 16)), -0.4, 0.0), -0.3, 0.3)
    mixing = jnp.clip(jnp.exp(math.log(5.0) - 4.6051702 * jax.random.uniform(seeds[2], (2, LEVELS - 1, NLAT, NLON), jnp.float32) ** block_levels(seeds[2], (2, LEVELS - 1, NLAT, NLON), ((0, 2), (2, 8), (3, 16)), -0.2, 0.2)), 0.05, 5.0)
    strip_source = draw_strip_source(jax.random.fold_in(seeds[6], 71), 0)
    strip_tile = set_ends(jax.random.randint(seeds[4], (2, NSTRIP), 0, NTILE), jax.random.fold_in(seeds[4], 1), 0, NTILE - 1).astype(jnp.int32)
    weights = centred(seeds[5], (2, NSTRIP, STRIP, TILE), (TILE // 4) ** -0.5, 1.5)
    return {"tracers": tracers, "winds": winds, "mixing": mixing, "strip_source": strip_source, "strip_tile": strip_tile, "weights": weights}


SIXTH = 1.0 / 6.0


def upwind_flux(courant, behind, upstream, downstream, beyond):
    rising = (5.0 * upstream + 2.0 * downstream - behind) * SIXTH
    falling = (2.0 * upstream + 5.0 * downstream - beyond) * SIXTH
    return jnp.maximum(courant, 0.0) * rising + jnp.minimum(courant, 0.0) * falling


def advect(padded, wind_pad):
    row_count = padded.shape[2] - 4
    col_count = padded.shape[3] - 4
    along_lon = padded[:, :, 2:row_count + 2, :]
    east_wind = wind_pad[0, :, 1:row_count + 1, :]
    face_east = 0.5 * (east_wind[:, :, 0:col_count + 1] + east_wind[:, :, 1:col_count + 2])
    flux_lon = upwind_flux(face_east, along_lon[..., 0:col_count + 1], along_lon[..., 1:col_count + 2],
                           along_lon[..., 2:col_count + 3], along_lon[..., 3:col_count + 4])
    along_lat = padded[:, :, :, 2:col_count + 2]
    north_wind = wind_pad[1, :, :, 1:col_count + 1]
    face_north = 0.5 * (north_wind[:, 0:row_count + 1, :] + north_wind[:, 1:row_count + 2, :])
    flux_lat = upwind_flux(face_north, along_lat[:, :, 0:row_count + 1, :], along_lat[:, :, 1:row_count + 2, :],
                           along_lat[:, :, 2:row_count + 3, :], along_lat[:, :, 3:row_count + 4, :])
    centre = padded[:, :, 2:row_count + 2, 2:col_count + 2]
    return centre - (flux_lon[..., 1:] - flux_lon[..., :-1]) - (flux_lat[:, :, 1:, :] - flux_lat[:, :, :-1, :])


def diffuse(column_field, mixing):
    level_count = column_field.shape[1]
    ratios = []
    partial_vals = []
    for height in range(level_count):
        diagonal = 1.0 + jnp.zeros_like(mixing[0])
        source_term = column_field[:, height]
        if height > 0:
            diagonal = diagonal + mixing[height - 1]
        if height < level_count - 1:
            diagonal = diagonal + mixing[height]
        if height > 0:
            pivot_value = diagonal - mixing[height - 1] * ratios[-1]
            source_term = source_term + mixing[height - 1] * partial_vals[-1]
        else:
            pivot_value = diagonal
        partial_vals.append(source_term / pivot_value)
        if height < level_count - 1:
            ratios.append(mixing[height] / pivot_value)
    solved = [partial_vals[-1]]
    for height in range(level_count - 2, -1, -1):
        solved.insert(0, partial_vals[height] + ratios[height] * solved[0])
    return jnp.stack(solved, axis=1)


def strip_values(source_panel, strip_source, strip_tile, weights):
    tile_columns = CLON // 16

    def one_strip(device_index, tile_index):
        row_start = (device_index // N_LON) * CLAT + (tile_index // tile_columns) * 4
        col_start = (device_index % N_LON) * CLON + (tile_index % tile_columns) * 16
        source_block = lax.dynamic_slice(
            source_panel, (jnp.int32(0), jnp.int32(0), row_start.astype(jnp.int32), col_start.astype(jnp.int32)),
            (TRACERS, LEVELS, 4, 16))
        return source_block.reshape(TRACERS * LEVELS, 64)

    tile_values = jax.vmap(one_strip)(strip_source, strip_tile)
    return jnp.einsum("sfk,sck->sfc", tile_values, weights.astype(jnp.float32), precision=lax.Precision.HIGHEST)


def fill_rim(panel_field, values):
    across_band = NLON // 16
    down_band = NLAT // 16

    def band_layout(strip_part):
        grid_view = strip_part.reshape(across_band, TRACERS, LEVELS, 2, 16)
        return jnp.transpose(grid_view, (1, 2, 3, 0, 4)).reshape(TRACERS, LEVELS, 2, NLON)

    def side_layout(strip_part):
        grid_view = strip_part.reshape(down_band, TRACERS, LEVELS, 16, 2)
        return jnp.transpose(grid_view, (1, 2, 0, 3, 4)).reshape(TRACERS, LEVELS, NLAT, 2)

    north_band = band_layout(values[0:across_band])
    south_band = band_layout(values[across_band:2 * across_band])
    west_band = side_layout(values[2 * across_band:2 * across_band + down_band])
    east_band = side_layout(values[2 * across_band + down_band:])
    panel_field = panel_field.at[:, :, :, 0:2].set(west_band)
    panel_field = panel_field.at[:, :, :, NLON - 2:].set(east_band)
    panel_field = panel_field.at[:, :, 0:2, :].set(north_band)
    panel_field = panel_field.at[:, :, NLAT - 2:, :].set(south_band)
    return panel_field


def reference(tracers, winds, mixing, strip_source, strip_tile, weights):
    tracer_state = tracers
    wind_pad = jnp.pad(winds, ((0, 0), (0, 0), (0, 0), (1, 1), (1, 1)))
    for step_number in range(STEPS):
        diffused = []
        for panel_index in range(2):
            padded = jnp.pad(tracer_state[panel_index], ((0, 0), (0, 0), (2, 2), (2, 2)))
            advanced = advect(padded, wind_pad[panel_index])
            diffused.append(diffuse(advanced, mixing[panel_index]))
        filled = []
        for panel_index in range(2):
            values = strip_values(diffused[1 - panel_index], strip_source[panel_index],
                                  strip_tile[panel_index], weights[panel_index])
            filled.append(fill_rim(diffused[panel_index], values))
        tracer_state = jnp.stack(filled)
    return tracer_state
```

```python
import functools

import jax
import jax.numpy as jnp
from jax import lax
from jax.experimental import pallas as pl
from jax.experimental.pallas import tpu as pltpu
from jax.sharding import PartitionSpec as P

MESH = pl.DeviceIdType.MESH
STEPS = 2
MIDS = 18
FIELDS = 72
LEVELS = 36
ROWS = 64
COLS = 128
SHARE = FIELDS // MIDS
PAD = 8
TALL = ROWS + 2 * PAD
CHUNK = 16
EAST, WEST, SOUTH, NORTH = range(4)


def mid_place(k):
    return 1 + k % 6, 1 + (5 * k) % 14


def kernel(lat_n, lon_n, tab, info, tr_hbm, wd_hbm, mix_hbm, wt_hbm, out_hbm,
           sa, sb, w0, w1, mx, cf, rt, wts, bd, pk, pkr, hp, rw, rwr, prev,
           pay, inb0, inb1, ob, rb, rs, dense, flip,
           lsem, ssem, rsem, p1s, p1r, p2s, p2bs, p2r, p2br):
    panel = lax.axis_index("panel")
    lat = lax.axis_index("lat")
    lon = lax.axis_index("lon")
    me = lat * lon_n + lon
    other = 1 - panel
    has = {
        EAST: lon < lon_n - 1,
        WEST: lon > 0,
        SOUTH: lat < lat_n - 1,
        NORTH: lat > 0,
    }
    beside = {
        EAST: (panel, lat, lon + 1),
        WEST: (panel, lat, lon - 1),
        SOUTH: (panel, lat + 1, lon),
        NORTH: (panel, lat - 1, lon),
    }
    is_band = (lat == 0) | (lat == lat_n - 1)
    is_side = (lon == 0) | (lon == lon_n - 1)
    mid_id = jnp.int32(-1)
    for k in range(MIDS):
        mlat, mlon = mid_place(k)
        mid_id = jnp.where((lat == mlat) & (lon == mlon), jnp.int32(k), mid_id)
    is_mid = mid_id >= 0
    inb = (inb0, inb1)
    lane8 = lax.broadcasted_iota(jnp.int32, (8, COLS), 1)
    lane_c = lax.broadcasted_iota(jnp.int32, (CHUNK, COLS), 1)

    loads = [
        pltpu.make_async_copy(tr_hbm, sa.at[:, pl.ds(PAD, ROWS), :], lsem.at[0]),
        pltpu.make_async_copy(wd_hbm.at[0], w0, lsem.at[1]),
        pltpu.make_async_copy(wd_hbm.at[1], w1.at[:, pl.ds(PAD, ROWS), :], lsem.at[2]),
        pltpu.make_async_copy(mix_hbm, mx.at[pl.ds(1, LEVELS - 1)], lsem.at[3]),
        pltpu.make_async_copy(wt_hbm.at[other], wts, lsem.at[4]),
    ]
    for load in loads:
        load.start()

    barrier = pltpu.get_barrier_semaphore()
    for way in range(4):
        @pl.when(has[way])
        def _():
            pl.semaphore_signal(barrier, inc=1, device_id=beside[way], device_id_type=MESH)

    @pl.when(is_mid)
    def _():
        def greet(i, carry):
            pl.semaphore_signal(
                barrier, inc=1, device_id=(other, i // lon_n, i % lon_n), device_id_type=MESH)
            return carry
        lax.fori_loop(0, lat_n * lon_n, greet, 0)

    def greet_mids():
        def greet(k, carry):
            mlat, mlon = mid_place(k)
            pl.semaphore_signal(
                barrier, inc=1, device_id=(panel, mlat, mlon), device_id_type=MESH)
            return carry
        lax.fori_loop(0, MIDS, greet, 0)

    pl.when(is_band)(greet_mids)
    pl.when(is_side)(greet_mids)
    one = jnp.int32(1)
    none = jnp.int32(0)
    expect = jnp.int32(MIDS)
    for way in range(4):
        expect = expect + jnp.where(has[way], one, none)
    expect = expect + jnp.where(is_mid, jnp.int32(2 * lon_n + 2 * lat_n), none)

    zero = jnp.zeros((ROWS, COLS), jnp.float32)
    mx[0] = zero
    mx[LEVELS] = zero
    rt[0] = zero
    bd[...] = jnp.zeros((128, 256), jnp.float32)
    for step in range(STEPS):
        for way in range(2):
            @pl.when(jnp.logical_not(has[way ^ 1]))
            def _():
                pkr[step, way] = jnp.zeros((4, ROWS, COLS), jnp.float32)

            @pl.when(jnp.logical_not(has[2 + (way ^ 1)]))
            def _():
                rwr[step, way] = jnp.zeros((FIELDS + LEVELS, 2, COLS), jnp.float32)
    loads[0].wait()
    loads[1].wait()
    loads[2].wait()

    def halo_copy(step, way):
        groups = 4 if step == 0 else 3
        fields = FIELDS + LEVELS if step == 0 else FIELDS
        if way in (EAST, WEST):
            src = pk.at[step, pl.ds(0, groups)]
            dst = pkr.at[step, way, pl.ds(0, groups)]
        else:
            src = rw.at[step, way - 2, pl.ds(0, fields)]
            dst = rwr.at[step, way - 2, pl.ds(0, fields)]
        return pltpu.make_async_remote_copy(
            src_ref=src, dst_ref=dst, send_sem=ssem.at[step, way], recv_sem=rsem.at[step, way],
            device_id=beside[way], device_id_type=MESH)

    def exchange(step, state):
        def pack(g, carry):
            rows = pl.ds(pl.multiple_of(PAD + g * 8, 8), 8)
            bare = pl.ds(pl.multiple_of(g * 8, 8), 8)
            count = FIELDS + LEVELS if step == 0 else FIELDS
            for group in range((count + 31) // 32):
                total = jnp.zeros((8, COLS), jnp.float32)
                for slot in range(min(32, count - 32 * group)):
                    f = 32 * group + slot
                    value = state[f, rows, :] if f < FIELDS else w0[f - FIELDS, bare, :]
                    moved = pltpu.roll(value, (4 * slot + 2) % COLS, 1)
                    total = jnp.where(lane8 // 4 == slot, moved, total)
                pk[step, group, bare, :] = total
            return carry
        lax.fori_loop(0, ROWS // 8, pack, 0)

        def rows_of(f, carry):
            rw[step, 0, f] = state[f, PAD + ROWS - 2:PAD + ROWS, :]
            rw[step, 1, f] = state[f, PAD:PAD + 2, :]
            return carry
        lax.fori_loop(0, FIELDS, rows_of, 0, unroll=8)
        if step == 0:
            def winds_of(l, carry):
                rw[step, 0, FIELDS + l] = w1[l, PAD + ROWS - 2:PAD + ROWS, :]
                rw[step, 1, FIELDS + l] = w1[l, PAD:PAD + 2, :]
                return carry
            lax.fori_loop(0, LEVELS, winds_of, 0, unroll=4)
            pl.semaphore_wait(barrier, expect)
        for way in range(4):
            @pl.when(has[way])
            def _():
                halo_copy(step, way).start()

    def take_halo(step, state):
        for way, came in ((EAST, WEST), (WEST, EAST), (SOUTH, NORTH), (NORTH, SOUTH)):
            @pl.when(has[came])
            def _():
                halo_copy(step, way).wait_recv()
        for group in range(4 if step == 0 else 3):
            for g in range(ROWS // CHUNK):
                rows = pl.ds(g * CHUNK, CHUNK)
                hp[group, rows, :] = jnp.where(
                    lane_c % 4 < 2, pkr[step, EAST, group, rows, :], pkr[step, WEST, group, rows, :])

        def rows_of(f, carry):
            state[f, PAD - 2:PAD, :] = rwr[step, 0, f]
            state[f, PAD + ROWS:PAD + ROWS + 2, :] = rwr[step, 1, f]
            return carry
        lax.fori_loop(0, FIELDS, rows_of, 0, unroll=8)
        if step == 0:
            def winds_of(l, carry):
                w1[l, PAD - 2:PAD, :] = rwr[step, 0, FIELDS + l]
                w1[l, PAD + ROWS:PAD + ROWS + 2, :] = rwr[step, 1, FIELDS + l]
                return carry
            lax.fori_loop(0, LEVELS, winds_of, 0, unroll=4)

    def sent_halo(step):
        for way in range(4):
            @pl.when(has[way])
            def _():
                halo_copy(step, way).wait_send()

    def halo_lanes(f, g):
        slot = f % 32
        return pltpu.roll(
            hp[f // 32, pl.ds(g * CHUNK, CHUNK), :], (2 * COLS - 2 - 4 * slot) % COLS, 1)

    def coefficients(l, carry):
        for g in range(ROWS // CHUNK):
            rows = pl.ds(g * CHUNK, CHUNK)
            w = w0[l, rows, :]
            beyond = halo_lanes(FIELDS + l, g)
            w_east = pltpu.roll(jnp.where(lane_c < 1, beyond, w), COLS - 1, 1)
            w_west = pltpu.roll(jnp.where(lane_c >= COLS - 1, beyond, w), 1, 1)
            base = PAD + g * CHUNK
            v = w1[l, base:base + CHUNK, :]
            v_next = w1[l, base + 1:base + CHUNK + 1, :]
            v_prev = w1[l, base - 1:base + CHUNK - 1, :]

            def parts(face):
                face = face * (1.0 / 12.0)
                return jnp.maximum(face, 0.0), jnp.minimum(face, 0.0)

            pe, me_ = parts(w + w_east)
            pw, mw = parts(w + w_west)
            pn, mn = parts(v + v_next)
            ps, ms = parts(v + v_prev)
            low = mx[l, rows, :]
            high = mx[l + 1, rows, :]
            pivot = 1.0 + low + high - low * rt[l, rows, :]
            inv = 1.0 / pivot
            rt[l + 1, rows, :] = high * inv
            centre = 1.0 + (2.0 * (pw - me_) + 5.0 * (mw - pe)) + (2.0 * (ps - mn) + 5.0 * (ms - pn))
            for i, c in enumerate((
                centre,
                -pw, 5.0 * pw + 2.0 * mw + pe, -mw - 2.0 * pe - 5.0 * me_, me_,
                -ps, 5.0 * ps + 2.0 * ms + pn, -ms - 2.0 * pn - 5.0 * mn, mn,
                low,
            )):
                cf[l, i, rows, :] = c * inv
        return carry

    def forward(state, new):
        prev[...] = jnp.zeros((2, ROWS, COLS), jnp.float32)

        def level(l, carry):
            for g in range(ROWS // CHUNK):
                rows = pl.ds(g * CHUNK, CHUNK)
                base = PAD + g * CHUNK
                for t in range(2):
                    f = t * LEVELS + l
                    q = state[f, base:base + CHUNK, :]
                    beyond = halo_lanes(f, g)
                    x = cf[l, 0, rows, :] * q
                    x += cf[l, 1, rows, :] * pltpu.roll(jnp.where(lane_c >= COLS - 2, beyond, q), 2, 1)
                    x += cf[l, 2, rows, :] * pltpu.roll(jnp.where(lane_c >= COLS - 1, beyond, q), 1, 1)
                    x += cf[l, 3, rows, :] * pltpu.roll(jnp.where(lane_c < 1, beyond, q), COLS - 1, 1)
                    x += cf[l, 4, rows, :] * pltpu.roll(jnp.where(lane_c < 2, beyond, q), COLS - 2, 1)
                    x += cf[l, 5, rows, :] * state[f, base - 2:base - 2 + CHUNK, :]
                    x += cf[l, 6, rows, :] * state[f, base - 1:base - 1 + CHUNK, :]
                    x += cf[l, 7, rows, :] * state[f, base + 1:base + 1 + CHUNK, :]
                    x += cf[l, 8, rows, :] * state[f, base + 2:base + 2 + CHUNK, :]
                    x += cf[l, 9, rows, :] * prev[t, rows, :]
                    prev[t, rows, :] = x
                    new[f, base:base + CHUNK, :] = x
            return carry
        lax.fori_loop(0, LEVELS, level, 0)

    def backward(new):
        def level(i, carry):
            l = LEVELS - 2 - i
            for g in range(ROWS // CHUNK):
                rows = pl.ds(g * CHUNK, CHUNK)
                base = PAD + g * CHUNK
                for t in range(2):
                    f = t * LEVELS + l
                    x = new[f, base:base + CHUNK, :] + rt[l + 1, rows, :] * prev[t, rows, :]
                    prev[t, rows, :] = x
                    new[f, base:base + CHUNK, :] = x
            return carry
        lax.fori_loop(0, LEVELS - 1, level, 0)

    def to_mid(step, k):
        mlat, mlon = mid_place(k)
        return pltpu.make_async_remote_copy(
            src_ref=pay.at[step, k], dst_ref=inb[step].at[me], send_sem=p1s.at[step],
            recv_sem=p1r.at[step], device_id=(other, mlat, mlon), device_id_type=MESH)

    def to_band(step, d):
        return pltpu.make_async_remote_copy(
            src_ref=ob.at[step, pl.ds(2 * d, 2)], dst_ref=rb.at[step, mid_id],
            send_sem=p2bs.at[step], recv_sem=p2br.at[step],
            device_id=(panel, (d // lon_n) * (lat_n - 1), d % lon_n), device_id_type=MESH)

    def to_side(step, e):
        return pltpu.make_async_remote_copy(
            src_ref=ob.at[step, 4 * lon_n + e], dst_ref=rs.at[step, mid_id],
            send_sem=p2s.at[step], recv_sem=p2r.at[step],
            device_id=(panel, e % lat_n, (e // lat_n) * (lon_n - 1)), device_id_type=MESH)

    def all_of(ref, sem):
        pltpu.make_async_copy(ref, ref, sem).wait()

    def provide(step, new):
        flat = new.reshape(FIELDS * TALL, COLS)
        lane_f = lax.broadcasted_iota(jnp.int32, (FIELDS, COLS), 1)
        total = jnp.zeros((FIELDS, COLS), jnp.float32)
        for pair in range(2):
            cells = jnp.zeros((FIELDS, COLS), jnp.float32)
            for s in range(2):
                tile = info[2 + 2 * pair + s]
                first = PAD + (tile // 8) * 4
                for r in range(4):
                    row = flat[pl.ds(first + r, FIELDS, stride=TALL), :]
                    shift = (2 * COLS + 64 * s + 16 * r - 16 * (tile % 8)) % COLS
                    row = pltpu.roll(row, shift, 1)
                    cells = jnp.where(lane_f // 16 == 4 * s + r, row, cells)
            w = bd[:, 128 * pair:128 * pair + 128].astype(jnp.bfloat16)
            rest = cells
            for part in range(3):
                piece = rest.astype(jnp.bfloat16)
                total += lax.dot_general(
                    piece, w, (((1,), (1,)), ((), ())), preferred_element_type=jnp.float32)
                if part < 2:
                    rest = rest - piece.astype(jnp.float32)
        for k in range(MIDS):
            pay[step, k] = total[SHARE * k:SHARE * k + SHARE, :]

        def send(k, carry):
            to_mid(step, k).start()
            return carry
        lax.fori_loop(0, MIDS, send, 0)

        @pl.when(is_mid)
        def _():
            all_of(inb[step], p1r.at[step])
            lane_s = lax.broadcasted_iota(jnp.int32, (SHARE, COLS), 1)
            batch = 8

            def sort(i, carry):
                done = []
                for j in range(batch):
                    u = i * batch + j
                    left = tab[2 * u]
                    right = tab[2 * u + 1]
                    a = pltpu.roll(inb[step][left // 2], (left % 2) * 64, 1)
                    b = pltpu.roll(inb[step][right // 2], 64 - (right % 2) * 64, 1)
                    done.append(jnp.where(lane_s < 64, a, b))
                for j in range(batch):
                    ob[step, i * batch + j] = done[j]
                return carry
            lax.fori_loop(0, (4 * lon_n + 2 * lat_n) // batch, sort, 0)

            def band(d, carry):
                to_band(step, d).start()
                return carry
            lax.fori_loop(0, 2 * lon_n, band, 0)

            def side(e, carry):
                to_side(step, e).start()
                return carry
            lax.fori_loop(0, 2 * lat_n, side, 0)

    def fill(step, new):
        @pl.when(is_side)
        def _():
            all_of(rs.at[step], p2r.at[step])
            for k in range(MIDS):
                dense[0, SHARE * k:SHARE * k + SHARE, :] = rs[step, k]
            flip[...] = jnp.transpose(dense[0])
            first = flip[pl.ds(0, ROWS, stride=2), :]
            second = flip[pl.ds(1, ROWS, stride=2), :]
            dense[0, 0:ROWS, :] = first
            dense[1, 0:ROWS, :] = second
            start = jnp.where(lon == 0, 0, COLS - 2)

            def column(f, carry):
                for g in range(ROWS // CHUNK):
                    rows = pl.ds(g * CHUNK, CHUNK)
                    base = PAD + g * CHUNK
                    a = pltpu.roll(dense[0, rows, :], (COLS + start - f) % COLS, 1)
                    b = pltpu.roll(dense[1, rows, :], (COLS + start + 1 - f) % COLS, 1)
                    q = new[f, base:base + CHUNK, :]
                    q = jnp.where(lane_c == start, a, q)
                    new[f, base:base + CHUNK, :] = jnp.where(lane_c == start + 1, b, q)
                return carry
            lax.fori_loop(0, FIELDS, column, 0, unroll=2)

        @pl.when(is_band)
        def _():
            all_of(rb.at[step], p2br.at[step])
            for k in range(MIDS):
                for u in range(2):
                    dense[u, SHARE * k:SHARE * k + SHARE, :] = rb[step, k, u]
            lane_f = lax.broadcasted_iota(jnp.int32, (FIELDS, COLS), 1)
            lines = []
            for r in range(2):
                line = jnp.zeros((FIELDS, COLS), jnp.float32)
                for u in range(2):
                    tiles = dense[u, 0:FIELDS, :]
                    for s in range(4):
                        moved = pltpu.roll(tiles, (2 * COLS + 64 * u - 16 * s - 16 * r) % COLS, 1)
                        line = jnp.where(lane_f // 16 == 4 * u + s, moved, line)
                lines.append(line)
            flat = new.reshape(FIELDS * TALL, COLS)
            for r in range(2):
                @pl.when(lat == 0)
                def _():
                    flat[pl.ds(PAD + r, FIELDS, stride=TALL), :] = lines[r]

                @pl.when(lat == lat_n - 1)
                def _():
                    flat[pl.ds(PAD + ROWS - 2 + r, FIELDS, stride=TALL), :] = lines[r]

    for step in range(STEPS):
        state, new = (sa, sb) if step % 2 == 0 else (sb, sa)
        exchange(step, state)
        if step == 0:
            loads[4].wait()
            for pair in range(2):
                for s in range(2):
                    b = 2 * pair + s
                    bd[32 * b:32 * b + 32, 64 * b:64 * b + 64] = wts[
                        2 * info[pair] + s].astype(jnp.float32)
            loads[3].wait()
        take_halo(step, state)
        if step == 0:
            lax.fori_loop(0, LEVELS, coefficients, 0)
        forward(state, new)
        backward(new)
        provide(step, new)
        fill(step, new)

    result = sa if STEPS % 2 == 0 else sb
    store = pltpu.make_async_copy(result.at[:, pl.ds(PAD, ROWS), :], out_hbm, lsem.at[0])
    store.start()
    for step in range(STEPS):
        sent_halo(step)
        all_of(pay.at[step], p1s.at[step])

        @pl.when(is_mid)
        def _():
            all_of(ob.at[step, pl.ds(0, 4 * lon_n)], p2bs.at[step])
            all_of(ob.at[step, pl.ds(4 * lon_n, 2 * lat_n)], p2s.at[step])
    store.wait()


def on_device(lat_n, lon_n, tracers, winds, mixing, strip_source, strip_tile, weights):
    panel = lax.axis_index("panel")
    me = lax.axis_index("lat") * lon_n + lax.axis_index("lon")
    sources = strip_source[:, ::2]
    pairs = sources.shape[1]
    order = jnp.arange(pairs, dtype=jnp.int32)
    same = (sources[:, :, None] == sources[:, None, :]) & (order[None, :] < order[:, None])[None]
    second = jnp.any(same, axis=2).astype(jnp.int32)
    tab = lax.dynamic_index_in_dim(sources * 2 + second, panel, 0, keepdims=False)
    theirs = lax.dynamic_index_in_dim(sources, 1 - panel, 0, keepdims=False)
    their_second = lax.dynamic_index_in_dim(second, 1 - panel, 0, keepdims=False)
    their_tile = lax.dynamic_index_in_dim(strip_tile, 1 - panel, 0, keepdims=False)
    mine = jnp.stack([jnp.where((theirs == me) & (their_second == h), 1, 0) for h in range(2)])
    ids = jnp.sum(mine * order, axis=1)
    tiles = jnp.sum(mine[:, :, None] * their_tile.reshape(1, pairs, 2), axis=1).reshape(4)
    info = jnp.concatenate([ids, tiles, jnp.zeros((2,), jnp.int32)]).astype(jnp.int32)
    f32 = jnp.float32
    vm = pltpu.VMEM
    dma = pltpu.SemaphoreType.DMA
    devices = lat_n * lon_n
    tiles_out = 4 * lon_n + 2 * lat_n
    anywhere = pl.BlockSpec(memory_space=pl.ANY)
    smem = pl.BlockSpec(memory_space=pltpu.SMEM)
    out = pl.pallas_call(
        functools.partial(kernel, lat_n, lon_n),
        out_shape=jax.ShapeDtypeStruct((FIELDS, ROWS, COLS), f32),
        in_specs=[smem, smem, anywhere, anywhere, anywhere, anywhere],
        out_specs=anywhere,
        scratch_shapes=[
            vm((FIELDS, TALL, COLS), f32),
            vm((FIELDS, TALL, COLS), f32),
            vm((LEVELS, ROWS, COLS), f32),
            vm((LEVELS, TALL, COLS), f32),
            vm((LEVELS + 1, ROWS, COLS), f32),
            vm((LEVELS, 10, ROWS, COLS), f32),
            vm((LEVELS + 1, ROWS, COLS), f32),
            vm(weights.shape[1:], weights.dtype),
            vm((128, 256), f32),
            vm((STEPS, 4, ROWS, COLS), f32),
            vm((STEPS, 2, 4, ROWS, COLS), f32),
            vm((4, ROWS, COLS), f32),
            vm((STEPS, 2, FIELDS + LEVELS, 2, COLS), f32),
            vm((STEPS, 2, FIELDS + LEVELS, 2, COLS), f32),
            vm((2, ROWS, COLS), f32),
            vm((STEPS, MIDS, SHARE, COLS), f32),
            vm((devices, SHARE, COLS), f32),
            vm((devices, SHARE, COLS), f32),
            vm((STEPS, tiles_out, SHARE, COLS), f32),
            vm((STEPS, MIDS, 2, SHARE, COLS), f32),
            vm((STEPS, MIDS, SHARE, COLS), f32),
            vm((2, 128, COLS), f32),
            vm((128, COLS), f32),
            dma((5,)),
            dma((STEPS, 4)),
            dma((STEPS, 4)),
            dma((STEPS,)),
            dma((STEPS,)),
            dma((STEPS,)),
            dma((STEPS,)),
            dma((STEPS,)),
            dma((STEPS,)),
        ],
        compiler_params=pltpu.CompilerParams(
            collective_id=0, has_side_effects=True, vmem_limit_bytes=56 * 1024 * 1024),
    )(
        tab, info,
        tracers.reshape(FIELDS, ROWS, COLS),
        winds.reshape(2, LEVELS, ROWS, COLS),
        mixing.reshape(LEVELS - 1, ROWS, COLS),
        weights,
    )
    return out.reshape(tracers.shape)


def solution(mesh):
    return jax.shard_map(
        functools.partial(on_device, mesh.shape["lat"], mesh.shape["lon"]),
        mesh=mesh,
        in_specs=(
            P("panel", None, None, "lat", "lon"),
            P("panel", None, None, "lat", "lon"),
            P("panel", None, "lat", "lon"),
            P(),
            P(),
            P(),
        ),
        out_specs=P("panel", None, None, "lat", "lon"),
        check_vma=False,
    )
```

```python
import functools

import jax
import jax.numpy as jnp
from jax import lax
from jax.experimental import pallas as pl
from jax.experimental.pallas import tpu as pltpu
from jax.sharding import PartitionSpec as P

MESH = pl.DeviceIdType.MESH
STEPS = 2
MIDS = 18
FIELDS = 72
LEVELS = 36
ROWS = 64
COLS = 128
SHARE = FIELDS // MIDS
PAD = 8
TALL = ROWS + 2 * PAD
CHUNK = 16
EAST, WEST, SOUTH, NORTH = range(4)


def mid_place(k):
    return 1 + k % 6, 1 + (5 * k) % 14


def kernel(lat_n, lon_n, ssrc, stile, vsrc, tr_hbm, wd_hbm, mix_hbm, wt_hbm, out_hbm,
           sa, sb, w0, w1, mx, cf, rt, iv, wts, bd, pk, pkr, hb, rw, rwr, prev,
           pay, inb0, inb1, hs, ob, rb, rs, dense, flip,
           lsem, ssem, rsem, p1s, p1r, p2s, p2bs, p2r, p2br):
    panel = lax.axis_index("panel")
    lat = lax.axis_index("lat")
    lon = lax.axis_index("lon")
    me = lat * lon_n + lon
    other = 1 - panel
    has = {
        EAST: lon < lon_n - 1,
        WEST: lon > 0,
        SOUTH: lat < lat_n - 1,
        NORTH: lat > 0,
    }
    beside = {
        EAST: (panel, lat, lon + 1),
        WEST: (panel, lat, lon - 1),
        SOUTH: (panel, lat + 1, lon),
        NORTH: (panel, lat - 1, lon),
    }
    is_band = (lat == 0) | (lat == lat_n - 1)
    is_side = (lon == 0) | (lon == lon_n - 1)
    mid_id = jnp.int32(-1)
    for k in range(MIDS):
        mlat, mlon = mid_place(k)
        mid_id = jnp.where((lat == mlat) & (lon == mlon), jnp.int32(k), mid_id)
    is_mid = mid_id >= 0
    inb = (inb0, inb1)
    lane8 = lax.broadcasted_iota(jnp.int32, (8, COLS), 1)
    lane_c = lax.broadcasted_iota(jnp.int32, (CHUNK, COLS), 1)

    loads = [
        pltpu.make_async_copy(tr_hbm, sa.at[:, pl.ds(PAD, ROWS), :], lsem.at[0]),
        pltpu.make_async_copy(wd_hbm.at[0], w0, lsem.at[1]),
        pltpu.make_async_copy(wd_hbm.at[1], w1.at[:, pl.ds(PAD, ROWS), :], lsem.at[2]),
        pltpu.make_async_copy(mix_hbm, mx.at[pl.ds(1, LEVELS - 1)], lsem.at[3]),
        pltpu.make_async_copy(wt_hbm.at[other], wts, lsem.at[4]),
    ]
    for load in loads[:3]:
        load.start()

    barrier = pltpu.get_barrier_semaphore()
    for way in range(4):
        @pl.when(has[way])
        def _():
            pl.semaphore_signal(barrier, inc=1, device_id=beside[way], device_id_type=MESH)

    @pl.when(is_mid)
    def _():
        def greet(i, carry):
            pl.semaphore_signal(
                barrier, inc=1, device_id=(other, i // lon_n, i % lon_n), device_id_type=MESH)
            return carry
        lax.fori_loop(0, lat_n * lon_n, greet, 0)

    def greet_mids():
        def greet(k, carry):
            mlat, mlon = mid_place(k)
            pl.semaphore_signal(
                barrier, inc=1, device_id=(panel, mlat, mlon), device_id_type=MESH)
            return carry
        lax.fori_loop(0, MIDS, greet, 0)

    pl.when(is_band)(greet_mids)
    pl.when(is_side)(greet_mids)
    one = jnp.int32(1)
    none = jnp.int32(0)
    expect = jnp.int32(MIDS)
    for way in range(4):
        expect = expect + jnp.where(has[way], one, none)
    expect = expect + jnp.where(is_mid, jnp.int32(2 * lon_n + 2 * lat_n), none)

    zero = jnp.zeros((ROWS, COLS), jnp.float32)
    mx[0] = zero
    mx[LEVELS] = zero
    rt[0] = zero
    for step in range(STEPS):
        for way in range(2):
            @pl.when(jnp.logical_not(has[way ^ 1]))
            def _():
                pkr[step, way] = jnp.zeros((4, ROWS, COLS), jnp.float32)

            @pl.when(jnp.logical_not(has[2 + (way ^ 1)]))
            def _():
                rwr[step, way] = jnp.zeros((FIELDS + LEVELS, 2, COLS), jnp.float32)

    def look(i, found):
        first, second = found
        for j in range(8):
            m = 8 * i + j
            hit = ssrc[other, 2 * m] == me
            second = jnp.where(hit & (first >= 0), m, second)
            first = jnp.where(hit & (first < 0), m, first)
        return first, second
    found = lax.fori_loop(0, ssrc.shape[1] // 16, look, (jnp.int32(-1), jnp.int32(-1)))
    found = [jnp.maximum(m, 0) for m in found]
    strips = [2 * m + s for m in found for s in range(2)]
    tiles = [stile[other, strip] for strip in strips]
    for load in loads[:3]:
        load.wait()
    for load in loads[3:]:
        load.start()

    def halo_copy(step, way):
        groups = 4 if step == 0 else 3
        fields = FIELDS + LEVELS if step == 0 else FIELDS
        if way in (EAST, WEST):
            src = pk.at[step, pl.ds(0, groups)]
            dst = pkr.at[step, way, pl.ds(0, groups)]
        else:
            src = rw.at[step, way - 2, pl.ds(0, fields)]
            dst = rwr.at[step, way - 2, pl.ds(0, fields)]
        return pltpu.make_async_remote_copy(
            src_ref=src, dst_ref=dst, send_sem=ssem.at[step, way], recv_sem=rsem.at[step, way],
            device_id=beside[way], device_id_type=MESH)

    def pack_halo(step, state):
        def pack(g, carry):
            rows = pl.ds(pl.multiple_of(PAD + g * 8, 8), 8)
            bare = pl.ds(pl.multiple_of(g * 8, 8), 8)
            count = FIELDS + LEVELS if step == 0 else FIELDS
            for group in range((count + 31) // 32):
                total = jnp.zeros((8, COLS), jnp.float32)
                for slot in range(min(32, count - 32 * group)):
                    f = 32 * group + slot
                    value = state[f, rows, :] if f < FIELDS else w0[f - FIELDS, bare, :]
                    moved = pltpu.roll(value, (4 * slot + 2) % COLS, 1)
                    total = jnp.where(lane8 // 4 == slot, moved, total)
                pk[step, group, bare, :] = total
            return carry
        lax.fori_loop(0, ROWS // 8, pack, 0)

        def rows_of(f, carry):
            rw[step, 0, f] = state[f, PAD + ROWS - 2:PAD + ROWS, :]
            rw[step, 1, f] = state[f, PAD:PAD + 2, :]
            return carry
        lax.fori_loop(0, FIELDS, rows_of, 0, unroll=8)
        if step == 0:
            def winds_of(l, carry):
                rw[step, 0, FIELDS + l] = w1[l, PAD + ROWS - 2:PAD + ROWS, :]
                rw[step, 1, FIELDS + l] = w1[l, PAD:PAD + 2, :]
                return carry
            lax.fori_loop(0, LEVELS, winds_of, 0, unroll=4)

    def send_halo(step):
        if step == 0:
            pl.semaphore_wait(barrier, expect)
        for way in range(4):
            @pl.when(has[way])
            def _():
                halo_copy(step, way).start()

    def wait_halo(step):
        for way, came in ((EAST, WEST), (WEST, EAST), (SOUTH, NORTH), (NORTH, SOUTH)):
            @pl.when(has[came])
            def _():
                halo_copy(step, way).wait_recv()

    def take_halo(step, state):
        def unpack(g, carry):
            rows = pl.ds(pl.multiple_of(g * 8, 8), 8)
            count = FIELDS + LEVELS if step == 0 else FIELDS
            for group in range((count + 31) // 32):
                both = jnp.where(
                    lane8 % 4 < 2, pkr[step, EAST, group, rows, :], pkr[step, WEST, group, rows, :])
                for slot in range(min(32, count - 32 * group)):
                    hb[32 * group + slot, rows, :] = pltpu.roll(
                        both, (2 * COLS - 2 - 4 * slot) % COLS, 1)
            return carry
        lax.fori_loop(0, ROWS // 8, unpack, 0)

        def rows_of(f, carry):
            state[f, PAD - 2:PAD, :] = rwr[step, 0, f]
            state[f, PAD + ROWS:PAD + ROWS + 2, :] = rwr[step, 1, f]
            return carry
        lax.fori_loop(0, FIELDS, rows_of, 0, unroll=8)
        if step == 0:
            def winds_of(l, carry):
                w1[l, PAD - 2:PAD, :] = rwr[step, 0, FIELDS + l]
                w1[l, PAD + ROWS:PAD + ROWS + 2, :] = rwr[step, 1, FIELDS + l]
                return carry
            lax.fori_loop(0, LEVELS, winds_of, 0, unroll=4)

    def sent_halo(step):
        for way in range(4):
            @pl.when(has[way])
            def _():
                halo_copy(step, way).wait_send()

    def pivots(l, carry):
        for g in range(ROWS // CHUNK):
            rows = pl.ds(g * CHUNK, CHUNK)
            low = mx[l, rows, :]
            high = mx[l + 1, rows, :]
            inv = 1.0 / (1.0 + low + high - low * rt[l, rows, :])
            iv[l, rows, :] = inv
            rt[l + 1, rows, :] = high * inv
            cf[l, 9, rows, :] = low * inv
        return carry

    def coefficients(l, carry):
        for g in range(ROWS // CHUNK):
            rows = pl.ds(g * CHUNK, CHUNK)
            w = w0[l, rows, :]
            beyond = hb[FIELDS + l, rows, :]
            w_east = pltpu.roll(jnp.where(lane_c < 1, beyond, w), COLS - 1, 1)
            w_west = pltpu.roll(jnp.where(lane_c >= COLS - 1, beyond, w), 1, 1)
            base = PAD + g * CHUNK
            v = w1[l, base:base + CHUNK, :]
            v_next = w1[l, base + 1:base + CHUNK + 1, :]
            v_prev = w1[l, base - 1:base + CHUNK - 1, :]

            def parts(face):
                face = face * (1.0 / 12.0)
                return jnp.maximum(face, 0.0), jnp.minimum(face, 0.0)

            pe, me_ = parts(w + w_east)
            pw, mw = parts(w + w_west)
            pn, mn = parts(v + v_next)
            ps, ms = parts(v + v_prev)
            inv = iv[l, rows, :]
            centre = 1.0 + (2.0 * (pw - me_) + 5.0 * (mw - pe)) + (2.0 * (ps - mn) + 5.0 * (ms - pn))
            for i, c in enumerate((
                centre,
                -pw, 5.0 * pw + 2.0 * mw + pe, -mw - 2.0 * pe - 5.0 * me_, me_,
                -ps, 5.0 * ps + 2.0 * ms + pn, -ms - 2.0 * pn - 5.0 * mn, mn,
            )):
                cf[l, i, rows, :] = c * inv
        return carry

    def forward(state, new):
        prev[...] = jnp.zeros((2, ROWS, COLS), jnp.float32)

        def level(l, carry):
            for g in range(ROWS // CHUNK):
                rows = pl.ds(g * CHUNK, CHUNK)
                base = PAD + g * CHUNK
                for t in range(2):
                    f = t * LEVELS + l
                    q = state[f, base:base + CHUNK, :]
                    beyond = hb[f, rows, :]
                    x = cf[l, 0, rows, :] * q
                    x += cf[l, 1, rows, :] * pltpu.roll(jnp.where(lane_c >= COLS - 2, beyond, q), 2, 1)
                    x += cf[l, 2, rows, :] * pltpu.roll(jnp.where(lane_c >= COLS - 1, beyond, q), 1, 1)
                    x += cf[l, 3, rows, :] * pltpu.roll(jnp.where(lane_c < 1, beyond, q), COLS - 1, 1)
                    x += cf[l, 4, rows, :] * pltpu.roll(jnp.where(lane_c < 2, beyond, q), COLS - 2, 1)
                    x += cf[l, 5, rows, :] * state[f, base - 2:base - 2 + CHUNK, :]
                    x += cf[l, 6, rows, :] * state[f, base - 1:base - 1 + CHUNK, :]
                    x += cf[l, 7, rows, :] * state[f, base + 1:base + 1 + CHUNK, :]
                    x += cf[l, 8, rows, :] * state[f, base + 2:base + 2 + CHUNK, :]
                    x += cf[l, 9, rows, :] * prev[t, rows, :]
                    prev[t, rows, :] = x
                    new[f, base:base + CHUNK, :] = x
            return carry
        lax.fori_loop(0, LEVELS, level, 0, unroll=2)

    def backward(new):
        def level(i, carry):
            l = LEVELS - 2 - i
            for g in range(ROWS // CHUNK):
                rows = pl.ds(g * CHUNK, CHUNK)
                base = PAD + g * CHUNK
                for t in range(2):
                    f = t * LEVELS + l
                    x = new[f, base:base + CHUNK, :] + rt[l + 1, rows, :] * prev[t, rows, :]
                    prev[t, rows, :] = x
                    new[f, base:base + CHUNK, :] = x
            return carry
        lax.fori_loop(0, LEVELS - 1, level, 0, unroll=5)

    def to_mid(step, k):
        mlat, mlon = mid_place(k)
        return pltpu.make_async_remote_copy(
            src_ref=pay.at[step, k], dst_ref=inb[step].at[me], send_sem=p1s.at[step],
            recv_sem=p1r.at[step], device_id=(other, mlat, mlon), device_id_type=MESH)

    def to_band(step, d):
        return pltpu.make_async_remote_copy(
            src_ref=ob.at[step, pl.ds(2 * d, 2)], dst_ref=rb.at[step, mid_id],
            send_sem=p2bs.at[step], recv_sem=p2br.at[step],
            device_id=(panel, (d // lon_n) * (lat_n - 1), d % lon_n), device_id_type=MESH)

    def to_side(step, e):
        return pltpu.make_async_remote_copy(
            src_ref=ob.at[step, 4 * lon_n + e], dst_ref=rs.at[step, mid_id],
            send_sem=p2s.at[step], recv_sem=p2r.at[step],
            device_id=(panel, e % lat_n, (e // lat_n) * (lon_n - 1)), device_id_type=MESH)

    def all_of(ref, sem):
        pltpu.make_async_copy(ref, ref, sem).wait()

    def provide(step, new):
        flat = new.reshape(FIELDS * TALL, COLS)
        lane_f = lax.broadcasted_iota(jnp.int32, (FIELDS, COLS), 1)
        total = jnp.zeros((FIELDS, COLS), jnp.float32)
        for pair in range(2):
            cells = jnp.zeros((FIELDS, COLS), jnp.float32)
            for s in range(2):
                tile = tiles[2 * pair + s]
                first = PAD + (tile // 8) * 4
                for r in range(4):
                    row = flat[pl.ds(first + r, FIELDS, stride=TALL), :]
                    shift = (2 * COLS + 64 * s + 16 * r - 16 * (tile % 8)) % COLS
                    row = pltpu.roll(row, shift, 1)
                    cells = jnp.where(lane_f // 16 == 4 * s + r, row, cells)
            w = bd[128 * pair:128 * pair + 128, :]
            rest = cells
            for part in range(3):
                piece = rest.astype(jnp.bfloat16)
                total += jnp.dot(piece, w, preferred_element_type=jnp.float32)
                if part < 2:
                    rest = rest - piece.astype(jnp.float32)
        for k in range(MIDS):
            pay[step, k] = total[SHARE * k:SHARE * k + SHARE, :]

    def route(step):
        def send(k, carry):
            to_mid(step, k).start()
            return carry
        lax.fori_loop(0, MIDS, send, 0)

        @pl.when(is_mid)
        def _():
            if step == 0:
                pairs = ssrc.shape[1] // 2
                shape = (pairs, 2 * pairs)
                row = jnp.where(panel == 0, vsrc[0:1, :], vsrc[1:2, :]).astype(jnp.float32)
                row = jnp.broadcast_to(row, shape)
                lane = lax.broadcasted_iota(jnp.int32, shape, 1)
                pair = lax.broadcasted_iota(jnp.int32, shape, 0)
                own = jnp.sum(jnp.where(lane == 2 * pair, row, 0.0), axis=1, keepdims=True)
                same = (row == own) & (lane % 2 == 0) & (lane < 2 * pair)
                second = jnp.max(jnp.where(same, 1.0, 0.0), axis=1, keepdims=True)
                hs[...] = jnp.broadcast_to(second, (pairs, COLS)).reshape(pairs // 8, 8, COLS)
            all_of(inb[step], p1r.at[step])
            lane_s = lax.broadcasted_iota(jnp.int32, (SHARE, COLS), 1)
            batch = 8

            def sort(i, carry):
                done = []
                for j in range(batch):
                    u = i * batch + j
                    a = inb[step][ssrc[panel, 4 * u]]
                    b = inb[step][ssrc[panel, 4 * u + 2]]
                    line = hs[2 * i + j // 4]
                    second_a = line[2 * j % 8:2 * j % 8 + 1, :] > 0.5
                    second_b = line[2 * j % 8 + 1:2 * j % 8 + 2, :] > 0.5
                    a = jnp.where(second_a, pltpu.roll(a, 64, 1), a)
                    b = jnp.where(second_b, b, pltpu.roll(b, 64, 1))
                    done.append(jnp.where(lane_s < 64, a, b))
                for j in range(batch):
                    ob[step, i * batch + j] = done[j]
                return carry
            lax.fori_loop(0, (4 * lon_n + 2 * lat_n) // batch, sort, 0)

            def band(d, carry):
                to_band(step, d).start()
                return carry
            lax.fori_loop(0, 2 * lon_n, band, 0)

            def side(e, carry):
                to_side(step, e).start()
                return carry
            lax.fori_loop(0, 2 * lat_n, side, 0)

    def fill(step, new):
        @pl.when(is_side)
        def _():
            all_of(rs.at[step], p2r.at[step])
            for k in range(MIDS):
                dense[0, SHARE * k:SHARE * k + SHARE, :] = rs[step, k]
            flip[...] = jnp.transpose(dense[0])
            first = flip[pl.ds(0, ROWS, stride=2), :]
            second = flip[pl.ds(1, ROWS, stride=2), :]
            start = jnp.where(lon == 0, 0, COLS - 2)
            dense[0, 0:ROWS, :] = pltpu.roll(first, start, 1)
            dense[1, 0:ROWS, :] = pltpu.roll(second, start + 1, 1)

            def column(g, carry):
                rows = pl.ds(pl.multiple_of(PAD + g * 8, 8), 8)
                bare = pl.ds(pl.multiple_of(g * 8, 8), 8)
                one, two = dense[0, bare, :], dense[1, bare, :]
                for f in range(FIELDS):
                    a = pltpu.roll(one, COLS - f, 1) if f else one
                    b = pltpu.roll(two, COLS - f, 1) if f else two
                    q = jnp.where(lane8 == start, a, new[f, rows, :])
                    new[f, rows, :] = jnp.where(lane8 == start + 1, b, q)
                return carry
            lax.fori_loop(0, ROWS // 8, column, 0)

        @pl.when(is_band)
        def _():
            all_of(rb.at[step], p2br.at[step])
            for k in range(MIDS):
                for u in range(2):
                    dense[u, SHARE * k:SHARE * k + SHARE, :] = rb[step, k, u]
            lane_f = lax.broadcasted_iota(jnp.int32, (FIELDS, COLS), 1)
            lines = []
            for r in range(2):
                line = jnp.zeros((FIELDS, COLS), jnp.float32)
                for u in range(2):
                    tiles = dense[u, 0:FIELDS, :]
                    for s in range(4):
                        moved = pltpu.roll(tiles, (2 * COLS + 64 * u - 16 * s - 16 * r) % COLS, 1)
                        line = jnp.where(lane_f // 16 == 4 * u + s, moved, line)
                lines.append(line)
            flat = new.reshape(FIELDS * TALL, COLS)
            for r in range(2):
                @pl.when(lat == 0)
                def _():
                    flat[pl.ds(PAD + r, FIELDS, stride=TALL), :] = lines[r]

                @pl.when(lat == lat_n - 1)
                def _():
                    flat[pl.ds(PAD + ROWS - 2 + r, FIELDS, stride=TALL), :] = lines[r]

    def pick_weights():
        entries = wts.shape[1]
        lane = lax.broadcasted_iota(jnp.int32, (entries, COLS), 1)
        wanted = jnp.zeros((entries, COLS), jnp.int32)
        for b in range(4):
            wanted = jnp.where(lane // 32 == b, strips[b], wanted)
        entry = lax.broadcasted_iota(jnp.int32, (entries, COLS), 0)
        one_hot = jnp.where(entry == wanted, 1.0, 0.0).astype(jnp.bfloat16)
        lane_k = lax.broadcasted_iota(jnp.int32, (64, COLS), 1)

        def cell(c, total):
            rows = wts[pl.ds(pl.multiple_of(c * 64, 64), 64), :]
            mine = jnp.dot(rows, one_hot, preferred_element_type=jnp.float32)
            return jnp.where(lane_k % 32 == c, mine, total)
        total = lax.fori_loop(0, 32, cell, jnp.zeros((64, COLS), jnp.float32), unroll=4)
        for b in range(4):
            bd[64 * b:64 * b + 64, :] = jnp.where(lane_k // 32 == b, total, 0.0).astype(jnp.bfloat16)

    for step in range(STEPS):
        state, new = (sa, sb) if step % 2 == 0 else (sb, sa)
        pack_halo(step, state)
        send_halo(step)
        if step == 0:
            loads[3].wait()
            lax.fori_loop(0, LEVELS, pivots, 0, unroll=2)
            loads[4].wait()
            pick_weights()
        wait_halo(step)
        take_halo(step, state)
        if step == 0:
            lax.fori_loop(0, LEVELS, coefficients, 0, unroll=2)
        forward(state, new)
        backward(new)
        provide(step, new)
        route(step)
        fill(step, new)

    result = sa if STEPS % 2 == 0 else sb
    store = pltpu.make_async_copy(result.at[:, pl.ds(PAD, ROWS), :], out_hbm, lsem.at[0])
    store.start()
    for step in range(STEPS):
        sent_halo(step)
        all_of(pay.at[step], p1s.at[step])

        @pl.when(is_mid)
        def _():
            all_of(ob.at[step, pl.ds(0, 4 * lon_n)], p2bs.at[step])
            all_of(ob.at[step, pl.ds(4 * lon_n, 2 * lat_n)], p2s.at[step])
    store.wait()


def on_device(lat_n, lon_n, tracers, winds, mixing, strip_source, strip_tile, weights):
    f32 = jnp.float32
    vm = pltpu.VMEM
    dma = pltpu.SemaphoreType.DMA
    devices = lat_n * lon_n
    tiles_out = 4 * lon_n + 2 * lat_n
    anywhere = pl.BlockSpec(memory_space=pl.ANY)
    smem = pl.BlockSpec(memory_space=pltpu.SMEM)
    out = pl.pallas_call(
        functools.partial(kernel, lat_n, lon_n),
        out_shape=jax.ShapeDtypeStruct((FIELDS, ROWS, COLS), f32),
        in_specs=[smem, smem, pl.BlockSpec(memory_space=pltpu.VMEM), anywhere, anywhere, anywhere, anywhere],
        out_specs=anywhere,
        scratch_shapes=[
            vm((FIELDS, TALL, COLS), f32),
            vm((FIELDS, TALL, COLS), f32),
            vm((LEVELS, ROWS, COLS), f32),
            vm((LEVELS, TALL, COLS), f32),
            vm((LEVELS + 1, ROWS, COLS), f32),
            vm((LEVELS, 10, ROWS, COLS), f32),
            vm((LEVELS + 1, ROWS, COLS), f32),
            vm((LEVELS, ROWS, COLS), f32),
            vm((32 * 64, weights.shape[1]), weights.dtype),
            vm((256, COLS), jnp.bfloat16),
            vm((STEPS, 4, ROWS, COLS), f32),
            vm((STEPS, 2, 4, ROWS, COLS), f32),
            vm((FIELDS + LEVELS, ROWS, COLS), f32),
            vm((STEPS, 2, FIELDS + LEVELS, 2, COLS), f32),
            vm((STEPS, 2, FIELDS + LEVELS, 2, COLS), f32),
            vm((2, ROWS, COLS), f32),
            vm((STEPS, MIDS, SHARE, COLS), f32),
            vm((devices, SHARE, COLS), f32),
            vm((devices, SHARE, COLS), f32),
            vm((strip_source.shape[1] // 16, 8, COLS), f32),
            vm((STEPS, tiles_out, SHARE, COLS), f32),
            vm((STEPS, MIDS, 2, SHARE, COLS), f32),
            vm((STEPS, MIDS, SHARE, COLS), f32),
            vm((2, 128, COLS), f32),
            vm((128, COLS), f32),
            dma((5,)),
            dma((STEPS, 4)),
            dma((STEPS, 4)),
            dma((STEPS,)),
            dma((STEPS,)),
            dma((STEPS,)),
            dma((STEPS,)),
            dma((STEPS,)),
            dma((STEPS,)),
        ],
        compiler_params=pltpu.CompilerParams(
            collective_id=0, has_side_effects=True, vmem_limit_bytes=56 * 1024 * 1024),
    )(
        strip_source, strip_tile, strip_source,
        tracers.reshape(FIELDS, ROWS, COLS),
        winds.reshape(2, LEVELS, ROWS, COLS),
        mixing.reshape(LEVELS - 1, ROWS, COLS),
        jnp.transpose(weights, (0, 2, 3, 1)).reshape(2, 32 * 64, weights.shape[1]),
    )
    return out.reshape(tracers.shape)


def solution(mesh):
    return jax.shard_map(
        functools.partial(on_device, mesh.shape["lat"], mesh.shape["lon"]),
        mesh=mesh,
        in_specs=(
            P("panel", None, None, "lat", "lon"),
            P("panel", None, None, "lat", "lon"),
            P("panel", None, "lat", "lon"),
            P(),
            P(),
            P(),
        ),
        out_specs=P("panel", None, None, "lat", "lon"),
        check_vma=False,
    )
```

```python
import functools

import jax
import jax.numpy as jnp
from jax import lax
from jax.experimental import pallas as pl
from jax.experimental.pallas import tpu as pltpu
from jax.sharding import PartitionSpec as P

MESH = pl.DeviceIdType.MESH
STEPS = 2
MIDS = 18
FIELDS = 72
LEVELS = 36
ROWS = 64
COLS = 128
SHARE = FIELDS // MIDS
PAD = 8
TALL = ROWS + 2 * PAD
CHUNK = 16
EAST, WEST, SOUTH, NORTH = range(4)


def mid_place(k):
    j = k // 2
    return 1 + 5 * (k % 2), 4 * (j // 2) + 1 + j % 2 - 9 * (j // 8)


def kernel(lat_n, lon_n, ssrc, stile, vsrc, tr_hbm, wd_hbm, mix_hbm, wt_hbm,
           out_hbm, sides_out, bands_out,
           sa, sb, w0, w1, mx, cf, rt, iv, wts, bd, pk, pkr, hb, rw, rwr, prev,
           pay, inb0, inb1, hs, ob, rb, rs, dense, flip,
           lsem, ssem, rsem, p1s, p1r, p2s, p2bs, p2r, p2br):
    panel = lax.axis_index("panel")
    lat = lax.axis_index("lat")
    lon = lax.axis_index("lon")
    me = lat * lon_n + lon
    other = 1 - panel
    has = {
        EAST: lon < lon_n - 1,
        WEST: lon > 0,
        SOUTH: lat < lat_n - 1,
        NORTH: lat > 0,
    }
    beside = {
        EAST: (panel, lat, lon + 1),
        WEST: (panel, lat, lon - 1),
        SOUTH: (panel, lat + 1, lon),
        NORTH: (panel, lat - 1, lon),
    }
    is_band = (lat == 0) | (lat == lat_n - 1)
    is_side = (lon == 0) | (lon == lon_n - 1)
    mid_id = jnp.int32(-1)
    for k in range(MIDS):
        mlat, mlon = mid_place(k)
        mid_id = jnp.where((lat == mlat) & (lon == mlon), jnp.int32(k), mid_id)
    is_mid = mid_id >= 0
    inb = (inb0, inb1)
    lane8 = lax.broadcasted_iota(jnp.int32, (8, COLS), 1)
    lane_c = lax.broadcasted_iota(jnp.int32, (CHUNK, COLS), 1)

    loads = [
        pltpu.make_async_copy(tr_hbm, sa.at[:, pl.ds(PAD, ROWS), :], lsem.at[0]),
        pltpu.make_async_copy(wd_hbm.at[0], w0, lsem.at[1]),
        pltpu.make_async_copy(wd_hbm.at[1], w1.at[:, pl.ds(PAD, ROWS), :], lsem.at[2]),
        pltpu.make_async_copy(mix_hbm, mx.at[pl.ds(1, LEVELS - 1)], lsem.at[3]),
        pltpu.make_async_copy(wt_hbm.at[other], wts, lsem.at[4]),
    ]
    for load in loads[:3]:
        load.start()

    barrier = pltpu.get_barrier_semaphore()
    for way in range(4):
        @pl.when(has[way])
        def _():
            pl.semaphore_signal(barrier, inc=1, device_id=beside[way], device_id_type=MESH)

    @pl.when(is_mid)
    def _():
        def greet(i, carry):
            pl.semaphore_signal(
                barrier, inc=1, device_id=(other, i // lon_n, i % lon_n), device_id_type=MESH)
            return carry
        lax.fori_loop(0, lat_n * lon_n, greet, 0)

    def greet_mids():
        def greet(k, carry):
            mlat, mlon = mid_place(k)
            pl.semaphore_signal(
                barrier, inc=1, device_id=(panel, mlat, mlon), device_id_type=MESH)
            return carry
        lax.fori_loop(0, MIDS, greet, 0)

    pl.when(is_band)(greet_mids)
    pl.when(is_side)(greet_mids)
    one = jnp.int32(1)
    none = jnp.int32(0)
    expect = jnp.int32(MIDS)
    for way in range(4):
        expect = expect + jnp.where(has[way], one, none)
    expect = expect + jnp.where(is_mid, jnp.int32(2 * lon_n + 2 * lat_n), none)

    zero = jnp.zeros((ROWS, COLS), jnp.float32)
    mx[0] = zero
    mx[LEVELS] = zero
    rt[0] = zero
    for step in range(STEPS):
        for way in range(2):
            @pl.when(jnp.logical_not(has[way ^ 1]))
            def _():
                pkr[step, way] = jnp.zeros((4, ROWS, COLS), jnp.float32)

            @pl.when(jnp.logical_not(has[2 + (way ^ 1)]))
            def _():
                rwr[step, way] = jnp.zeros((FIELDS + LEVELS, 2, COLS), jnp.float32)

    def look(i, found):
        first, second = found
        for j in range(8):
            m = 8 * i + j
            hit = ssrc[other, 2 * m] == me
            second = jnp.where(hit & (first >= 0), m, second)
            first = jnp.where(hit & (first < 0), m, first)
        return first, second
    found = lax.fori_loop(0, ssrc.shape[1] // 16, look, (jnp.int32(-1), jnp.int32(-1)))
    found = [jnp.maximum(m, 0) for m in found]
    strips = [2 * m + s for m in found for s in range(2)]
    tiles = [stile[other, strip] for strip in strips]
    for load in loads[:3]:
        load.wait()
    for load in loads[3:]:
        load.start()

    def fields_of(step):
        return FIELDS + LEVELS if step == 0 else FIELDS

    def groups_of(step):
        return (fields_of(step) + 31) // 32

    def rows_copy(step, way):
        part = pl.ds(0, fields_of(step))
        return pltpu.make_async_remote_copy(
            src_ref=rw.at[step, way - 2, part], dst_ref=rwr.at[step, way - 2, part],
            send_sem=ssem.at[step, way, 0], recv_sem=rsem.at[step, way, 0],
            device_id=beside[way], device_id_type=MESH)

    def columns_copy(step, way, group):
        return pltpu.make_async_remote_copy(
            src_ref=pk.at[step, group], dst_ref=pkr.at[step, way, group],
            send_sem=ssem.at[step, way, group], recv_sem=rsem.at[step, way, group],
            device_id=beside[way], device_id_type=MESH)

    def send_columns(step, group):
        for way in (EAST, WEST):
            @pl.when(has[way])
            def _():
                columns_copy(step, way, group).start()

    def pack_columns(step, state, group):
        def pack(g, carry):
            rows = pl.ds(pl.multiple_of(PAD + g * 8, 8), 8)
            bare = pl.ds(pl.multiple_of(g * 8, 8), 8)
            total = jnp.zeros((8, COLS), jnp.float32)
            for slot in range(min(32, fields_of(step) - 32 * group)):
                f = 32 * group + slot
                value = state[f, rows, :] if f < FIELDS else w0[f - FIELDS, bare, :]
                moved = pltpu.roll(value, (4 * slot + 2) % COLS, 1)
                total = jnp.where(lane8 // 4 == slot, moved, total)
            pk[step, group, bare, :] = total
            return carry
        lax.fori_loop(0, ROWS // 8, pack, 0, unroll=2)

    def give_halo(step, state):
        def rows_of(f, carry):
            rw[step, 0, f] = state[f, PAD + ROWS - 2:PAD + ROWS, :]
            rw[step, 1, f] = state[f, PAD:PAD + 2, :]
            return carry
        lax.fori_loop(0, FIELDS, rows_of, 0, unroll=8)
        if step == 0:
            def winds_of(l, carry):
                rw[step, 0, FIELDS + l] = w1[l, PAD + ROWS - 2:PAD + ROWS, :]
                rw[step, 1, FIELDS + l] = w1[l, PAD:PAD + 2, :]
                return carry
            lax.fori_loop(0, LEVELS, winds_of, 0, unroll=4)
        pack_columns(step, state, 0)
        if step == 0:
            pl.semaphore_wait(barrier, expect)
        send_columns(step, 0)
        for way in (SOUTH, NORTH):
            @pl.when(has[way])
            def _():
                rows_copy(step, way).start()
        for group in range(1, groups_of(step)):
            pack_columns(step, state, group)
            send_columns(step, group)

    def take_halo(step, state):
        for way, came in ((SOUTH, NORTH), (NORTH, SOUTH)):
            @pl.when(has[came])
            def _():
                rows_copy(step, way).wait_recv()

        def rows_of(f, carry):
            state[f, PAD - 2:PAD, :] = rwr[step, 0, f]
            state[f, PAD + ROWS:PAD + ROWS + 2, :] = rwr[step, 1, f]
            return carry
        lax.fori_loop(0, FIELDS, rows_of, 0, unroll=8)
        if step == 0:
            def winds_of(l, carry):
                w1[l, PAD - 2:PAD, :] = rwr[step, 0, FIELDS + l]
                w1[l, PAD + ROWS:PAD + ROWS + 2, :] = rwr[step, 1, FIELDS + l]
                return carry
            lax.fori_loop(0, LEVELS, winds_of, 0, unroll=4)
        for group in range(groups_of(step)):
            for way, came in ((EAST, WEST), (WEST, EAST)):
                @pl.when(has[came])
                def _():
                    columns_copy(step, way, group).wait_recv()

            def unpack(g, carry):
                rows = pl.ds(pl.multiple_of(g * 8, 8), 8)
                both = jnp.where(
                    lane8 % 4 < 2, pkr[step, EAST, group, rows, :], pkr[step, WEST, group, rows, :])
                for slot in range(min(32, fields_of(step) - 32 * group)):
                    hb[32 * group + slot, rows, :] = pltpu.roll(
                        both, (2 * COLS - 2 - 4 * slot) % COLS, 1)
                return carry
            lax.fori_loop(0, ROWS // 8, unpack, 0, unroll=2)

    def sent_halo(step):
        for way in range(4):
            @pl.when(has[way])
            def _():
                if way in (EAST, WEST):
                    for group in range(groups_of(step)):
                        columns_copy(step, way, group).wait_send()
                else:
                    rows_copy(step, way).wait_send()

    def pivots(l, carry):
        for g in range(ROWS // CHUNK):
            rows = pl.ds(g * CHUNK, CHUNK)
            low = mx[l, rows, :]
            high = mx[l + 1, rows, :]
            inv = 1.0 / (1.0 + low + high - low * rt[l, rows, :])
            iv[l, rows, :] = inv
            rt[l + 1, rows, :] = high * inv
            cf[l, 9, rows, :] = low * inv
        return carry

    def coefficients(l, carry):
        for g in range(ROWS // CHUNK):
            rows = pl.ds(g * CHUNK, CHUNK)
            w = w0[l, rows, :]
            beyond = hb[FIELDS + l, rows, :]
            w_east = pltpu.roll(jnp.where(lane_c < 1, beyond, w), COLS - 1, 1)
            w_west = pltpu.roll(jnp.where(lane_c >= COLS - 1, beyond, w), 1, 1)
            base = PAD + g * CHUNK
            v = w1[l, base:base + CHUNK, :]
            v_next = w1[l, base + 1:base + CHUNK + 1, :]
            v_prev = w1[l, base - 1:base + CHUNK - 1, :]

            def parts(face):
                face = face * (1.0 / 12.0)
                return jnp.maximum(face, 0.0), jnp.minimum(face, 0.0)

            pe, me_ = parts(w + w_east)
            pw, mw = parts(w + w_west)
            pn, mn = parts(v + v_next)
            ps, ms = parts(v + v_prev)
            inv = iv[l, rows, :]
            centre = 1.0 + (2.0 * (pw - me_) + 5.0 * (mw - pe)) + (2.0 * (ps - mn) + 5.0 * (ms - pn))
            for i, c in enumerate((
                centre,
                -pw, 5.0 * pw + 2.0 * mw + pe, -mw - 2.0 * pe - 5.0 * me_, me_,
                -ps, 5.0 * ps + 2.0 * ms + pn, -ms - 2.0 * pn - 5.0 * mn, mn,
            )):
                cf[l, i, rows, :] = c * inv
        return carry

    def forward(state, new):
        prev[...] = jnp.zeros((2, ROWS, COLS), jnp.float32)

        def level(l, carry):
            for g in range(ROWS // CHUNK):
                rows = pl.ds(g * CHUNK, CHUNK)
                base = PAD + g * CHUNK
                for t in range(2):
                    f = t * LEVELS + l
                    q = state[f, base:base + CHUNK, :]
                    beyond = hb[f, rows, :]
                    x = cf[l, 0, rows, :] * q
                    x += cf[l, 1, rows, :] * pltpu.roll(jnp.where(lane_c >= COLS - 2, beyond, q), 2, 1)
                    x += cf[l, 2, rows, :] * pltpu.roll(jnp.where(lane_c >= COLS - 1, beyond, q), 1, 1)
                    x += cf[l, 3, rows, :] * pltpu.roll(jnp.where(lane_c < 1, beyond, q), COLS - 1, 1)
                    x += cf[l, 4, rows, :] * pltpu.roll(jnp.where(lane_c < 2, beyond, q), COLS - 2, 1)
                    x += cf[l, 5, rows, :] * state[f, base - 2:base - 2 + CHUNK, :]
                    x += cf[l, 6, rows, :] * state[f, base - 1:base - 1 + CHUNK, :]
                    x += cf[l, 7, rows, :] * state[f, base + 1:base + 1 + CHUNK, :]
                    x += cf[l, 8, rows, :] * state[f, base + 2:base + 2 + CHUNK, :]
                    x += cf[l, 9, rows, :] * prev[t, rows, :]
                    prev[t, rows, :] = x
                    new[f, base:base + CHUNK, :] = x
            return carry
        lax.fori_loop(0, LEVELS, level, 0, unroll=2)

    def backward(new):
        def level(i, carry):
            l = LEVELS - 2 - i
            for g in range(ROWS // CHUNK):
                rows = pl.ds(g * CHUNK, CHUNK)
                base = PAD + g * CHUNK
                for t in range(2):
                    f = t * LEVELS + l
                    x = new[f, base:base + CHUNK, :] + rt[l + 1, rows, :] * prev[t, rows, :]
                    prev[t, rows, :] = x
                    new[f, base:base + CHUNK, :] = x
            return carry
        lax.fori_loop(0, LEVELS - 1, level, 0, unroll=5)

    def to_mid(step, k):
        mlat, mlon = mid_place(k)
        return pltpu.make_async_remote_copy(
            src_ref=pay.at[step, k], dst_ref=inb[step].at[me], send_sem=p1s.at[step],
            recv_sem=p1r.at[step], device_id=(other, mlat, mlon), device_id_type=MESH)

    def to_band(step, d):
        return pltpu.make_async_remote_copy(
            src_ref=ob.at[step, pl.ds(2 * d, 2)], dst_ref=rb.at[step, mid_id],
            send_sem=p2bs.at[step], recv_sem=p2br.at[step],
            device_id=(panel, (d // lon_n) * (lat_n - 1), d % lon_n), device_id_type=MESH)

    def to_side(step, e):
        return pltpu.make_async_remote_copy(
            src_ref=ob.at[step, 4 * lon_n + e], dst_ref=rs.at[step, mid_id],
            send_sem=p2s.at[step], recv_sem=p2r.at[step],
            device_id=(panel, e % lat_n, (e // lat_n) * (lon_n - 1)), device_id_type=MESH)

    def all_of(ref, sem):
        pltpu.make_async_copy(ref, ref, sem).wait()

    def provide(step, new):
        flat = new.reshape(FIELDS * TALL, COLS)
        lane_f = lax.broadcasted_iota(jnp.int32, (FIELDS, COLS), 1)
        total = jnp.zeros((FIELDS, COLS), jnp.float32)
        for pair in range(2):
            cells = jnp.zeros((FIELDS, COLS), jnp.float32)
            for s in range(2):
                tile = tiles[2 * pair + s]
                first = PAD + (tile // 8) * 4
                for r in range(4):
                    row = flat[pl.ds(first + r, FIELDS, stride=TALL), :]
                    shift = (2 * COLS + 64 * s + 16 * r - 16 * (tile % 8)) % COLS
                    row = pltpu.roll(row, shift, 1)
                    cells = jnp.where(lane_f // 16 == 4 * s + r, row, cells)
            w = bd[128 * pair:128 * pair + 128, :]
            rest = cells
            for part in range(3):
                piece = rest.astype(jnp.bfloat16)
                total += jnp.dot(piece, w, preferred_element_type=jnp.float32)
                if part < 2:
                    rest = rest - piece.astype(jnp.float32)
        for k in range(MIDS):
            pay[step, k] = total[SHARE * k:SHARE * k + SHARE, :]

    def route(step):
        def send(k, carry):
            to_mid(step, k).start()
            return carry
        lax.fori_loop(0, MIDS, send, 0)

        @pl.when(is_mid)
        def _():
            if step == 0:
                pairs = ssrc.shape[1] // 2
                shape = (pairs, 2 * pairs)
                row = jnp.where(panel == 0, vsrc[0:1, :], vsrc[1:2, :]).astype(jnp.float32)
                row = jnp.broadcast_to(row, shape)
                lane = lax.broadcasted_iota(jnp.int32, shape, 1)
                pair = lax.broadcasted_iota(jnp.int32, shape, 0)
                own = jnp.sum(jnp.where(lane == 2 * pair, row, 0.0), axis=1, keepdims=True)
                same = (row == own) & (lane % 2 == 0) & (lane < 2 * pair)
                second = jnp.max(jnp.where(same, 1.0, 0.0), axis=1, keepdims=True)
                hs[...] = jnp.broadcast_to(second, (pairs, COLS)).reshape(pairs // 8, 8, COLS)
            all_of(inb[step], p1r.at[step])
            lane_s = lax.broadcasted_iota(jnp.int32, (SHARE, COLS), 1)
            batch = 8

            def sort(i):
                done = []
                for j in range(batch):
                    u = i * batch + j
                    a = inb[step][ssrc[panel, 4 * u]]
                    b = inb[step][ssrc[panel, 4 * u + 2]]
                    line = hs[2 * i + j // 4]
                    second_a = line[2 * j % 8:2 * j % 8 + 1, :] > 0.5
                    second_b = line[2 * j % 8 + 1:2 * j % 8 + 2, :] > 0.5
                    a = jnp.where(second_a, pltpu.roll(a, 64, 1), a)
                    b = jnp.where(second_b, b, pltpu.roll(b, 64, 1))
                    done.append(jnp.where(lane_s < 64, a, b))
                for j in range(batch):
                    ob[step, i * batch + j] = done[j]

            def sides(i, carry):
                sort(4 * lon_n // batch + i)
                for j in range(batch):
                    to_side(step, batch * i + j).start()
                return carry
            lax.fori_loop(0, 2 * lat_n // batch, sides, 0)

            def bands(i, carry):
                sort(i)
                for j in range(batch // 2):
                    to_band(step, batch // 2 * i + j).start()
                return carry
            lax.fori_loop(0, 4 * lon_n // batch, bands, 0)

    def side_lines(step):
        all_of(rs.at[step], p2r.at[step])
        for k in range(MIDS):
            dense[0, SHARE * k:SHARE * k + SHARE, :] = rs[step, k]
        flip[...] = jnp.transpose(dense[0])
        first = flip[pl.ds(0, ROWS, stride=2), :]
        second = pltpu.roll(flip[pl.ds(1, ROWS, stride=2), :], 1, 1)
        even = lax.broadcasted_iota(jnp.int32, (ROWS, COLS), 1) % 2 == 0
        start = jnp.where(lon == 0, 0, COLS - 2)
        return (pltpu.roll(jnp.where(even, first, second), start, 1),
                pltpu.roll(jnp.where(even, second, first), start, 1))

    def band_lines(step):
        all_of(rb.at[step], p2br.at[step])
        for k in range(MIDS):
            for u in range(2):
                dense[u, SHARE * k:SHARE * k + SHARE, :] = rb[step, k, u]
        lane_f = lax.broadcasted_iota(jnp.int32, (FIELDS, COLS), 1)
        lines = []
        for r in range(2):
            line = jnp.zeros((FIELDS, COLS), jnp.float32)
            for u in range(2):
                tiles = dense[u, 0:FIELDS, :]
                for s in range(4):
                    moved = pltpu.roll(tiles, (2 * COLS + 64 * u - 16 * s - 16 * r) % COLS, 1)
                    line = jnp.where(lane_f // 16 == 4 * u + s, moved, line)
            lines.append(line)
        return lines

    def fill(step, new):
        @pl.when(is_side)
        def _():
            dense[0, 0:ROWS, :], dense[1, 0:ROWS, :] = side_lines(step)
            start = jnp.where(lon == 0, 0, COLS - 2)

            def column(g, carry):
                rows = pl.ds(pl.multiple_of(PAD + g * 8, 8), 8)
                bare = pl.ds(pl.multiple_of(g * 8, 8), 8)
                pair = dense[0, bare, :], dense[1, bare, :]
                for f in range(FIELDS):
                    a = pltpu.roll(pair[f % 2], COLS - f, 1) if f else pair[0]
                    new[f, rows, :] = jnp.where(lane8 // 2 == start // 2, a, new[f, rows, :])
                return carry
            lax.fori_loop(0, ROWS // 8, column, 0)

        @pl.when(is_band)
        def _():
            lines = band_lines(step)
            flat = new.reshape(FIELDS * TALL, COLS)
            for r in range(2):
                @pl.when(lat == 0)
                def _():
                    flat[pl.ds(PAD + r, FIELDS, stride=TALL), :] = lines[r]

                @pl.when(lat == lat_n - 1)
                def _():
                    flat[pl.ds(PAD + ROWS - 2 + r, FIELDS, stride=TALL), :] = lines[r]

    def hand_on(step):
        @pl.when(is_side)
        def _():
            sides_out[0], sides_out[1] = side_lines(step)

        @pl.when(is_band)
        def _():
            bands_out[0], bands_out[1] = band_lines(step)

    def pick_weights():
        entries = wts.shape[1]
        lane = lax.broadcasted_iota(jnp.int32, (entries, COLS), 1)
        wanted = jnp.zeros((entries, COLS), jnp.int32)
        for b in range(4):
            wanted = jnp.where(lane // 32 == b, strips[b], wanted)
        entry = lax.broadcasted_iota(jnp.int32, (entries, COLS), 0)
        one_hot = jnp.where(entry == wanted, 1.0, 0.0).astype(jnp.bfloat16)
        lane_k = lax.broadcasted_iota(jnp.int32, (64, COLS), 1)

        def cell(c, total):
            rows = wts[pl.ds(pl.multiple_of(c * 64, 64), 64), :]
            mine = jnp.dot(rows, one_hot, preferred_element_type=jnp.float32)
            return jnp.where(lane_k % 32 == c, mine, total)
        total = lax.fori_loop(0, 32, cell, jnp.zeros((64, COLS), jnp.float32), unroll=4)
        for b in range(4):
            bd[64 * b:64 * b + 64, :] = jnp.where(lane_k // 32 == b, total, 0.0).astype(jnp.bfloat16)

    for step in range(STEPS):
        state, new = (sa, sb) if step % 2 == 0 else (sb, sa)
        give_halo(step, state)
        if step == 0:
            loads[3].wait()
            lax.fori_loop(0, LEVELS, pivots, 0, unroll=2)
            loads[4].wait()
            pick_weights()
        take_halo(step, state)
        if step == 0:
            lax.fori_loop(0, LEVELS, coefficients, 0, unroll=2)
        forward(state, new)
        backward(new)
        if step == STEPS - 1:
            store = pltpu.make_async_copy(new.at[:, pl.ds(PAD, ROWS), :], out_hbm, lsem.at[0])
            store.start()
        provide(step, new)
        route(step)
        if step < STEPS - 1:
            fill(step, new)
        else:
            hand_on(step)

    for step in range(STEPS):
        sent_halo(step)
        all_of(pay.at[step], p1s.at[step])

        @pl.when(is_mid)
        def _():
            all_of(ob.at[step, pl.ds(0, 4 * lon_n)], p2bs.at[step])
            all_of(ob.at[step, pl.ds(4 * lon_n, 2 * lat_n)], p2s.at[step])
    store.wait()


def last_fill(lat_n, lon_n, state, sides, bands, out):
    lat = lax.axis_index("lat")
    lon = lax.axis_index("lon")
    count = state.shape[0]
    is_side = (lon == 0) | (lon == lon_n - 1)

    @pl.when(jnp.logical_not(is_side))
    def _():
        out[...] = state[...]

    @pl.when(is_side)
    def _():
        start = jnp.where(lon == 0, 0, COLS - 2)
        lane = lax.broadcasted_iota(jnp.int32, (ROWS, COLS), 1)
        first = count * pl.program_id(0)
        for j in range(count):
            a = pltpu.roll(sides[j % 2], (COLS - first - j) % COLS, 1)
            out[j] = jnp.where(lane // 2 == start // 2, a, state[j])

    for edge, row in ((0, 0), (lat_n - 1, ROWS - 2)):
        @pl.when(lat == edge)
        def _():
            for j in range(count):
                for r in range(2):
                    out[j, row + r:row + r + 1, :] = bands[r, j:j + 1, :]


def on_device(lat_n, lon_n, tracers, winds, mixing, strip_source, strip_tile, weights):
    f32 = jnp.float32
    vm = pltpu.VMEM
    dma = pltpu.SemaphoreType.DMA
    devices = lat_n * lon_n
    tiles_out = 4 * lon_n + 2 * lat_n
    anywhere = pl.BlockSpec(memory_space=pl.ANY)
    smem = pl.BlockSpec(memory_space=pltpu.SMEM)
    in_vmem = pl.BlockSpec(memory_space=pltpu.VMEM)
    state, sides, bands = pl.pallas_call(
        functools.partial(kernel, lat_n, lon_n),
        out_shape=(
            jax.ShapeDtypeStruct((FIELDS, ROWS, COLS), f32),
            jax.ShapeDtypeStruct((2, ROWS, COLS), f32),
            jax.ShapeDtypeStruct((2, FIELDS, COLS), f32),
        ),
        in_specs=[smem, smem, in_vmem, anywhere, anywhere, anywhere, anywhere],
        out_specs=(anywhere, in_vmem, in_vmem),
        scratch_shapes=[
            vm((FIELDS, TALL, COLS), f32),
            vm((FIELDS, TALL, COLS), f32),
            vm((LEVELS, ROWS, COLS), f32),
            vm((LEVELS, TALL, COLS), f32),
            vm((LEVELS + 1, ROWS, COLS), f32),
            vm((LEVELS, 10, ROWS, COLS), f32),
            vm((LEVELS + 1, ROWS, COLS), f32),
            vm((LEVELS, ROWS, COLS), f32),
            vm((32 * 64, weights.shape[1]), weights.dtype),
            vm((256, COLS), jnp.bfloat16),
            vm((STEPS, 4, ROWS, COLS), f32),
            vm((STEPS, 2, 4, ROWS, COLS), f32),
            vm((FIELDS + LEVELS, ROWS, COLS), f32),
            vm((STEPS, 2, FIELDS + LEVELS, 2, COLS), f32),
            vm((STEPS, 2, FIELDS + LEVELS, 2, COLS), f32),
            vm((2, ROWS, COLS), f32),
            vm((STEPS, MIDS, SHARE, COLS), f32),
            vm((devices, SHARE, COLS), f32),
            vm((devices, SHARE, COLS), f32),
            vm((strip_source.shape[1] // 16, 8, COLS), f32),
            vm((STEPS, tiles_out, SHARE, COLS), f32),
            vm((STEPS, MIDS, 2, SHARE, COLS), f32),
            vm((STEPS, MIDS, SHARE, COLS), f32),
            vm((2, 128, COLS), f32),
            vm((128, COLS), f32),
            dma((5,)),
            dma((STEPS, 4, 4)),
            dma((STEPS, 4, 4)),
            dma((STEPS,)),
            dma((STEPS,)),
            dma((STEPS,)),
            dma((STEPS,)),
            dma((STEPS,)),
            dma((STEPS,)),
        ],
        compiler_params=pltpu.CompilerParams(
            collective_id=0, has_side_effects=True, vmem_limit_bytes=56 * 1024 * 1024),
    )(
        strip_source, strip_tile, strip_source,
        tracers.reshape(FIELDS, ROWS, COLS),
        winds.reshape(2, LEVELS, ROWS, COLS),
        mixing.reshape(LEVELS - 1, ROWS, COLS),
        jnp.transpose(weights, (0, 2, 3, 1)).reshape(2, 32 * 64, weights.shape[1]),
    )
    some = FIELDS // 3
    block = pl.BlockSpec((some, ROWS, COLS), lambda i: (i, 0, 0))
    out = pl.pallas_call(
        functools.partial(last_fill, lat_n, lon_n),
        grid=(3,),
        out_shape=jax.ShapeDtypeStruct((FIELDS, ROWS, COLS), f32),
        in_specs=[
            block,
            pl.BlockSpec((2, ROWS, COLS), lambda i: (0, 0, 0)),
            pl.BlockSpec((2, some, COLS), lambda i: (0, i, 0)),
        ],
        out_specs=block,
        compiler_params=pltpu.CompilerParams(vmem_limit_bytes=56 * 1024 * 1024),
    )(state, sides, bands)
    return out.reshape(tracers.shape)


def solution(mesh):
    return jax.shard_map(
        functools.partial(on_device, mesh.shape["lat"], mesh.shape["lon"]),
        mesh=mesh,
        in_specs=(
            P("panel", None, None, "lat", "lon"),
            P("panel", None, None, "lat", "lon"),
            P("panel", None, "lat", "lon"),
            P(),
            P(),
            P(),
        ),
        out_specs=P("panel", None, None, "lat", "lon"),
        check_vma=False,
    )
```

```python
import functools

import jax
import jax.numpy as jnp
from jax import lax
from jax.experimental import pallas as pl
from jax.experimental.pallas import tpu as pltpu
from jax.sharding import PartitionSpec as P

MESH = pl.DeviceIdType.MESH
STEPS = 2
MIDS = 9
FIELDS = 72
LEVELS = 36
ROWS = 64
COLS = 128
SHARE = FIELDS // MIDS
PAD = 8
TALL = ROWS + 2 * PAD
CHUNK = 16
EAST, WEST, SOUTH, NORTH = range(4)


def mid_place(k):
    j = k // 2
    return 1 + 5 * (k % 2), 4 * (j // 2) + 1 + j % 2 - 9 * (j // 8)


def kernel(lat_n, lon_n, ssrc, stile, vsrc, tr_hbm, wd_hbm, mix_hbm, wt_hbm,
           out_hbm, sides_out, bands_out,
           sa, sb, w0, w1, mx, cf, rt, iv, wts, bd, pk, pkr, pt, ptr, hb, rw, rwr, prev,
           pay, inb0, inb1, hs, ob, rb, rs, dense, flip,
           lsem, ssem, rsem, psem, p1s, p1r, p2s, p2bs, p2r, p2br):
    panel = lax.axis_index("panel")
    lat = lax.axis_index("lat")
    lon = lax.axis_index("lon")
    me = lat * lon_n + lon
    other = 1 - panel
    has = {
        EAST: lon < lon_n - 1,
        WEST: lon > 0,
        SOUTH: lat < lat_n - 1,
        NORTH: lat > 0,
    }
    beside = {
        EAST: (panel, lat, lon + 1),
        WEST: (panel, lat, lon - 1),
        SOUTH: (panel, lat + 1, lon),
        NORTH: (panel, lat - 1, lon),
    }
    is_band = (lat == 0) | (lat == lat_n - 1)
    is_side = (lon == 0) | (lon == lon_n - 1)
    mid_id = jnp.int32(-1)
    for k in range(MIDS):
        mlat, mlon = mid_place(k)
        mid_id = jnp.where((lat == mlat) & (lon == mlon), jnp.int32(k), mid_id)
    is_mid = mid_id >= 0
    inb = (inb0, inb1)
    lane8 = lax.broadcasted_iota(jnp.int32, (8, COLS), 1)
    lane_c = lax.broadcasted_iota(jnp.int32, (CHUNK, COLS), 1)

    early = 64
    loads = [
        pltpu.make_async_copy(wd_hbm.at[0], w0, lsem.at[0]),
        pltpu.make_async_copy(
            tr_hbm.at[pl.ds(early, FIELDS - early)],
            sa.at[pl.ds(early, FIELDS - early), pl.ds(PAD, ROWS), :], lsem.at[1]),
        pltpu.make_async_copy(
            tr_hbm.at[pl.ds(0, early)], sa.at[pl.ds(0, early), pl.ds(PAD, ROWS), :], lsem.at[2]),
        pltpu.make_async_copy(wd_hbm.at[1], w1.at[:, pl.ds(PAD, ROWS), :], lsem.at[3]),
        pltpu.make_async_copy(mix_hbm, mx.at[pl.ds(1, LEVELS - 1)], lsem.at[4]),
        pltpu.make_async_copy(wt_hbm.at[other], wts, lsem.at[5]),
    ]
    for load in loads[:4]:
        load.start()

    barrier = pltpu.get_barrier_semaphore()
    for way in range(4):
        @pl.when(has[way])
        def _():
            pl.semaphore_signal(barrier, inc=1, device_id=beside[way], device_id_type=MESH)

    @pl.when(is_mid)
    def _():
        def greet(i, carry):
            pl.semaphore_signal(
                barrier, inc=1, device_id=(other, i // lon_n, i % lon_n), device_id_type=MESH)
            return carry
        lax.fori_loop(0, lat_n * lon_n, greet, 0)

    def greet_mids():
        def greet(k, carry):
            mlat, mlon = mid_place(k)
            pl.semaphore_signal(
                barrier, inc=1, device_id=(panel, mlat, mlon), device_id_type=MESH)
            return carry
        lax.fori_loop(0, MIDS, greet, 0)

    pl.when(is_band)(greet_mids)
    pl.when(is_side)(greet_mids)
    one = jnp.int32(1)
    none = jnp.int32(0)
    expect = jnp.int32(MIDS)
    for way in range(4):
        expect = expect + jnp.where(has[way], one, none)
    expect = expect + jnp.where(is_mid, jnp.int32(2 * lon_n + 2 * lat_n), none)

    zero = jnp.zeros((ROWS, COLS), jnp.float32)
    mx[0] = zero
    mx[LEVELS] = zero
    rt[0] = zero
    for step in range(STEPS):
        for way in range(2):
            @pl.when(jnp.logical_not(has[way ^ 1]))
            def _():
                pkr[step, way] = jnp.zeros((4, ROWS, COLS), jnp.float32)

            @pl.when(jnp.logical_not(has[2 + (way ^ 1)]))
            def _():
                rwr[step, way] = jnp.zeros((FIELDS + LEVELS, 2, COLS), jnp.float32)
    for way in range(2):
        @pl.when(jnp.logical_not(has[way ^ 1]))
        def _():
            ptr[way] = jnp.zeros((3, 8, COLS), jnp.float32)

    def look(i, found):
        first, second = found
        for j in range(8):
            m = 8 * i + j
            hit = ssrc[other, 2 * m] == me
            second = jnp.where(hit & (first >= 0), m, second)
            first = jnp.where(hit & (first < 0), m, first)
        return first, second
    found = lax.fori_loop(0, ssrc.shape[1] // 16, look, (jnp.int32(-1), jnp.int32(-1)))
    found = [jnp.maximum(m, 0) for m in found]
    strips = [2 * m + s for m in found for s in range(2)]
    tiles = [stile[other, strip] for strip in strips]
    loads[0].wait()
    loads[1].wait()
    loads[4].start()
    loads[5].start()

    def fields_of(step):
        return FIELDS + LEVELS if step == 0 else FIELDS

    def groups_of(step):
        return (fields_of(step) + 31) // 32

    def rows_copy(step, way):
        part = pl.ds(0, fields_of(step))
        return pltpu.make_async_remote_copy(
            src_ref=rw.at[step, way - 2, part], dst_ref=rwr.at[step, way - 2, part],
            send_sem=ssem.at[step, way, 0], recv_sem=rsem.at[step, way, 0],
            device_id=beside[way], device_id_type=MESH)

    def columns_copy(step, way, group):
        return pltpu.make_async_remote_copy(
            src_ref=pk.at[step, group], dst_ref=pkr.at[step, way, group],
            send_sem=ssem.at[step, way, group], recv_sem=rsem.at[step, way, group],
            device_id=beside[way], device_id_type=MESH)

    def send_columns(step, group):
        for way in (EAST, WEST):
            @pl.when(has[way])
            def _():
                columns_copy(step, way, group).start()

    def packed(step, state, group, g):
        rows = pl.ds(pl.multiple_of(PAD + g * 8, 8), 8)
        bare = pl.ds(pl.multiple_of(g * 8, 8), 8)
        total = jnp.zeros((8, COLS), jnp.float32)
        for slot in range(min(32, fields_of(step) - 32 * group)):
            f = 32 * group + slot
            value = state[f, rows, :] if f < FIELDS else w0[f - FIELDS, bare, :]
            moved = pltpu.roll(value, (4 * slot + 2) % COLS, 1)
            total = jnp.where(lane8 // 4 == slot, moved, total)
        return total

    def unpacked(step, group, g, from_west, from_east):
        both = jnp.where(lane8 % 4 < 2, from_west, from_east)
        rows = pl.ds(pl.multiple_of(g * 8, 8), 8)
        for slot in range(min(32, fields_of(step) - 32 * group)):
            hb[32 * group + slot, rows, :] = pltpu.roll(both, (2 * COLS - 2 - 4 * slot) % COLS, 1)

    def pack_columns(step, state, group):
        def pack(g, carry):
            pk[step, group, pl.ds(pl.multiple_of(g * 8, 8), 8), :] = packed(step, state, group, g)
            return carry
        lax.fori_loop(0, ROWS // 8, pack, 0, unroll=2)

    def give_rows(step, state):
        def rows_of(f, carry):
            rw[step, 0, f] = state[f, PAD + ROWS - 2:PAD + ROWS, :]
            rw[step, 1, f] = state[f, PAD:PAD + 2, :]
            return carry
        lax.fori_loop(0, FIELDS, rows_of, 0, unroll=8)
        if step == 0:
            def winds_of(l, carry):
                rw[step, 0, FIELDS + l] = w1[l, PAD + ROWS - 2:PAD + ROWS, :]
                rw[step, 1, FIELDS + l] = w1[l, PAD:PAD + 2, :]
                return carry
            lax.fori_loop(0, LEVELS, winds_of, 0, unroll=4)
        for way in (SOUTH, NORTH):
            @pl.when(has[way])
            def _():
                rows_copy(step, way).start()

    def give_first_halo(state):
        pack_columns(0, state, 2)
        pl.semaphore_wait(barrier, expect)
        send_columns(0, 2)
        pack_columns(0, state, 3)
        send_columns(0, 3)
        loads[2].wait()
        loads[3].wait()
        give_rows(0, state)
        for group in range(2):
            pack_columns(0, state, group)
            send_columns(0, group)

    def take_rows(step, state):
        for way, came in ((SOUTH, NORTH), (NORTH, SOUTH)):
            @pl.when(has[came])
            def _():
                rows_copy(step, way).wait_recv()

        def rows_of(f, carry):
            state[f, PAD - 2:PAD, :] = rwr[step, 0, f]
            state[f, PAD + ROWS:PAD + ROWS + 2, :] = rwr[step, 1, f]
            return carry
        lax.fori_loop(0, FIELDS, rows_of, 0, unroll=8)
        if step == 0:
            def winds_of(l, carry):
                w1[l, PAD - 2:PAD, :] = rwr[step, 0, FIELDS + l]
                w1[l, PAD + ROWS:PAD + ROWS + 2, :] = rwr[step, 1, FIELDS + l]
                return carry
            lax.fori_loop(0, LEVELS, winds_of, 0, unroll=4)
    def take_columns(step, groups):
        for group in groups:
            for way, came in ((EAST, WEST), (WEST, EAST)):
                @pl.when(has[came])
                def _():
                    columns_copy(step, way, group).wait_recv()

            def unpack(g, carry):
                rows = pl.ds(pl.multiple_of(g * 8, 8), 8)
                unpacked(step, group, g, pkr[step, EAST, group, rows, :], pkr[step, WEST, group, rows, :])
                return carry
            lax.fori_loop(0, ROWS // 8, unpack, 0, unroll=2)

    def patch_copy(way):
        return pltpu.make_async_remote_copy(
            src_ref=pt, dst_ref=ptr.at[way], send_sem=psem.at[0, way], recv_sem=psem.at[1, way],
            device_id=beside[way], device_id_type=MESH)

    def patch_columns(step, state):
        for edge, g in ((0, 0), (lat_n - 1, ROWS // 8 - 1)):
            @pl.when(lat == edge)
            def _():
                for group in range(3):
                    pt[group] = packed(step, state, group, g)
        for way in (EAST, WEST):
            @pl.when(has[way])
            def _():
                patch_copy(way).start()
        for way in (EAST, WEST):
            @pl.when(has[way ^ 1])
            def _():
                patch_copy(way).wait_recv()
        for edge, g in ((0, 0), (lat_n - 1, ROWS // 8 - 1)):
            @pl.when(lat == edge)
            def _():
                for group in range(3):
                    unpacked(step, group, g, ptr[EAST, group], ptr[WEST, group])

    def sent_halo(step):
        for way in range(4):
            @pl.when(has[way])
            def _():
                if way in (EAST, WEST):
                    for group in range(groups_of(step)):
                        columns_copy(step, way, group).wait_send()
                    if step > 0:
                        pl.when(is_band)(patch_copy(way).wait_send)
                else:
                    rows_copy(step, way).wait_send()

    def pivots(l, carry):
        for g in range(ROWS // CHUNK):
            rows = pl.ds(g * CHUNK, CHUNK)
            low = mx[l, rows, :]
            high = mx[l + 1, rows, :]
            inv = 1.0 / (1.0 + low + high - low * rt[l, rows, :])
            iv[l, rows, :] = inv
            rt[l + 1, rows, :] = high * inv
            cf[l, 9, rows, :] = low * inv
        return carry

    def coefficients(l, carry):
        for g in range(ROWS // CHUNK):
            rows = pl.ds(g * CHUNK, CHUNK)
            w = w0[l, rows, :]
            beyond = hb[FIELDS + l, rows, :]
            w_east = pltpu.roll(jnp.where(lane_c < 1, beyond, w), COLS - 1, 1)
            w_west = pltpu.roll(jnp.where(lane_c >= COLS - 1, beyond, w), 1, 1)
            base = PAD + g * CHUNK
            v = w1[l, base:base + CHUNK, :]
            v_next = w1[l, base + 1:base + CHUNK + 1, :]
            v_prev = w1[l, base - 1:base + CHUNK - 1, :]

            def parts(face):
                face = face * (1.0 / 12.0)
                return jnp.maximum(face, 0.0), jnp.minimum(face, 0.0)

            pe, me_ = parts(w + w_east)
            pw, mw = parts(w + w_west)
            pn, mn = parts(v + v_next)
            ps, ms = parts(v + v_prev)
            inv = iv[l, rows, :]
            centre = 1.0 + (2.0 * (pw - me_) + 5.0 * (mw - pe)) + (2.0 * (ps - mn) + 5.0 * (ms - pn))
            for i, c in enumerate((
                centre,
                -pw, 5.0 * pw + 2.0 * mw + pe, -mw - 2.0 * pe - 5.0 * me_, me_,
                -ps, 5.0 * ps + 2.0 * ms + pn, -ms - 2.0 * pn - 5.0 * mn, mn,
            )):
                cf[l, i, rows, :] = c * inv
        return carry

    def forward(state, new):
        prev[...] = jnp.zeros((2, ROWS, COLS), jnp.float32)

        def level(l, carry):
            for g in range(ROWS // CHUNK):
                rows = pl.ds(g * CHUNK, CHUNK)
                base = PAD + g * CHUNK
                for t in range(2):
                    f = t * LEVELS + l
                    q = state[f, base:base + CHUNK, :]
                    beyond = hb[f, rows, :]
                    x = cf[l, 0, rows, :] * q
                    x += cf[l, 1, rows, :] * pltpu.roll(jnp.where(lane_c >= COLS - 2, beyond, q), 2, 1)
                    x += cf[l, 2, rows, :] * pltpu.roll(jnp.where(lane_c >= COLS - 1, beyond, q), 1, 1)
                    x += cf[l, 3, rows, :] * pltpu.roll(jnp.where(lane_c < 1, beyond, q), COLS - 1, 1)
                    x += cf[l, 4, rows, :] * pltpu.roll(jnp.where(lane_c < 2, beyond, q), COLS - 2, 1)
                    x += cf[l, 5, rows, :] * state[f, base - 2:base - 2 + CHUNK, :]
                    x += cf[l, 6, rows, :] * state[f, base - 1:base - 1 + CHUNK, :]
                    x += cf[l, 7, rows, :] * state[f, base + 1:base + 1 + CHUNK, :]
                    x += cf[l, 8, rows, :] * state[f, base + 2:base + 2 + CHUNK, :]
                    x += cf[l, 9, rows, :] * prev[t, rows, :]
                    prev[t, rows, :] = x
                    new[f, base:base + CHUNK, :] = x
            return carry
        lax.fori_loop(0, LEVELS, level, 0, unroll=2)

    def backward(new):
        def level(i, carry):
            l = LEVELS - 2 - i
            for g in range(ROWS // CHUNK):
                rows = pl.ds(g * CHUNK, CHUNK)
                base = PAD + g * CHUNK
                for t in range(2):
                    f = t * LEVELS + l
                    x = new[f, base:base + CHUNK, :] + rt[l + 1, rows, :] * prev[t, rows, :]
                    prev[t, rows, :] = x
                    new[f, base:base + CHUNK, :] = x
            return carry
        lax.fori_loop(0, LEVELS - 1, level, 0, unroll=5)

    def to_mid(step, k):
        mlat, mlon = mid_place(k)
        return pltpu.make_async_remote_copy(
            src_ref=pay.at[step, k], dst_ref=inb[step].at[me], send_sem=p1s.at[step],
            recv_sem=p1r.at[step], device_id=(other, mlat, mlon), device_id_type=MESH)

    def to_band(step, d):
        return pltpu.make_async_remote_copy(
            src_ref=ob.at[step, pl.ds(2 * d, 2)], dst_ref=rb.at[step, mid_id],
            send_sem=p2bs.at[step], recv_sem=p2br.at[step],
            device_id=(panel, (d // lon_n) * (lat_n - 1), d % lon_n), device_id_type=MESH)

    def to_side(step, e):
        return pltpu.make_async_remote_copy(
            src_ref=ob.at[step, 4 * lon_n + e], dst_ref=rs.at[step, mid_id],
            send_sem=p2s.at[step], recv_sem=p2r.at[step],
            device_id=(panel, e % lat_n, (e // lat_n) * (lon_n - 1)), device_id_type=MESH)

    def all_of(ref, sem):
        pltpu.make_async_copy(ref, ref, sem).wait()

    def provide(step, new):
        flat = new.reshape(FIELDS * TALL, COLS)
        lane_f = lax.broadcasted_iota(jnp.int32, (FIELDS, COLS), 1)
        total = jnp.zeros((FIELDS, COLS), jnp.float32)
        for pair in range(2):
            cells = jnp.zeros((FIELDS, COLS), jnp.float32)
            for s in range(2):
                tile = tiles[2 * pair + s]
                first = PAD + (tile // 8) * 4
                for r in range(4):
                    row = flat[pl.ds(first + r, FIELDS, stride=TALL), :]
                    shift = (2 * COLS + 64 * s + 16 * r - 16 * (tile % 8)) % COLS
                    row = pltpu.roll(row, shift, 1)
                    cells = jnp.where(lane_f // 16 == 4 * s + r, row, cells)
            w = bd[128 * pair:128 * pair + 128, :]
            rest = cells
            for part in range(3):
                piece = rest.astype(jnp.bfloat16)
                total += jnp.dot(piece, w, preferred_element_type=jnp.float32)
                if part < 2:
                    rest = rest - piece.astype(jnp.float32)
        pay[step] = total.reshape(MIDS, SHARE, COLS)

    def route(step):
        def send(k, carry):
            to_mid(step, k).start()
            return carry
        lax.fori_loop(0, MIDS, send, 0)

    def sort_and_send(step):
        @pl.when(is_mid)
        def _():
            if step == 0:
                pairs = ssrc.shape[1] // 2
                shape = (pairs, 2 * pairs)
                row = jnp.where(panel == 0, vsrc[0:1, :], vsrc[1:2, :]).astype(jnp.float32)
                row = jnp.broadcast_to(row, shape)
                lane = lax.broadcasted_iota(jnp.int32, shape, 1)
                pair = lax.broadcasted_iota(jnp.int32, shape, 0)
                own = jnp.sum(jnp.where(lane == 2 * pair, row, 0.0), axis=1, keepdims=True)
                same = (row == own) & (lane % 2 == 0) & (lane < 2 * pair)
                second = jnp.max(jnp.where(same, 1.0, 0.0), axis=1, keepdims=True)
                hs[...] = jnp.broadcast_to(second, (pairs, COLS)).reshape(pairs // 8, 8, COLS)
            all_of(inb[step], p1r.at[step])
            lane_s = lax.broadcasted_iota(jnp.int32, (SHARE, COLS), 1)
            batch = 8

            def sort(i):
                done = []
                for j in range(batch):
                    u = i * batch + j
                    a = inb[step][ssrc[panel, 4 * u]]
                    b = inb[step][ssrc[panel, 4 * u + 2]]
                    line = hs[2 * i + j // 4]
                    second_a = line[2 * j % 8:2 * j % 8 + 1, :] > 0.5
                    second_b = line[2 * j % 8 + 1:2 * j % 8 + 2, :] > 0.5
                    a = jnp.where(second_a, pltpu.roll(a, 64, 1), a)
                    b = jnp.where(second_b, b, pltpu.roll(b, 64, 1))
                    done.append(jnp.where(lane_s < 64, a, b))
                for j in range(batch):
                    ob[step, i * batch + j] = done[j]

            def sides(i, carry):
                sort(4 * lon_n // batch + i)
                for j in range(batch):
                    to_side(step, batch * i + j).start()
                return carry
            lax.fori_loop(0, 2 * lat_n // batch, sides, 0)

            def bands(i, carry):
                sort(i)
                for j in range(batch // 2):
                    to_band(step, batch // 2 * i + j).start()
                return carry
            lax.fori_loop(0, 4 * lon_n // batch, bands, 0)

    def side_lines(step):
        all_of(rs.at[step], p2r.at[step])
        dense[0, 0:FIELDS, :] = rs[step].reshape(FIELDS, COLS)
        flip[...] = jnp.transpose(dense[0])
        first = flip[pl.ds(0, ROWS, stride=2), :]
        second = pltpu.roll(flip[pl.ds(1, ROWS, stride=2), :], 1, 1)
        even = lax.broadcasted_iota(jnp.int32, (ROWS, COLS), 1) % 2 == 0
        start = jnp.where(lon == 0, 0, COLS - 2)
        return (pltpu.roll(jnp.where(even, first, second), start, 1),
                pltpu.roll(jnp.where(even, second, first), start, 1))

    def band_lines(step):
        all_of(rb.at[step], p2br.at[step])
        lane_f = lax.broadcasted_iota(jnp.int32, (FIELDS, COLS), 1)
        lines = []
        for r in range(2):
            line = jnp.zeros((FIELDS, COLS), jnp.float32)
            for u in range(2):
                tiles = rb[step, :, u].reshape(FIELDS, COLS)
                for s in range(4):
                    moved = pltpu.roll(tiles, (2 * COLS + 64 * u - 16 * s - 16 * r) % COLS, 1)
                    line = jnp.where(lane_f // 16 == 4 * u + s, moved, line)
            lines.append(line)
        return lines

    def fill(step, new):
        @pl.when(is_side)
        def _():
            dense[0, 0:ROWS, :], dense[1, 0:ROWS, :] = side_lines(step)
            start = jnp.where(lon == 0, 0, COLS - 2)

            def column(g, carry):
                rows = pl.ds(pl.multiple_of(PAD + g * 8, 8), 8)
                bare = pl.ds(pl.multiple_of(g * 8, 8), 8)
                pair = dense[0, bare, :], dense[1, bare, :]
                for f in range(FIELDS):
                    a = pltpu.roll(pair[f % 2], COLS - f, 1) if f else pair[0]
                    new[f, rows, :] = jnp.where(lane8 // 2 == start // 2, a, new[f, rows, :])
                return carry
            lax.fori_loop(0, ROWS // 8, column, 0)

        @pl.when(is_band)
        def _():
            lines = band_lines(step)
            flat = new.reshape(FIELDS * TALL, COLS)
            for r in range(2):
                @pl.when(lat == 0)
                def _():
                    flat[pl.ds(PAD + r, FIELDS, stride=TALL), :] = lines[r]

                @pl.when(lat == lat_n - 1)
                def _():
                    flat[pl.ds(PAD + ROWS - 2 + r, FIELDS, stride=TALL), :] = lines[r]

    def hand_on(step):
        @pl.when(is_side)
        def _():
            sides_out[0], sides_out[1] = side_lines(step)

        @pl.when(is_band)
        def _():
            bands_out[0], bands_out[1] = band_lines(step)

    def pick_weights():
        entries = wts.shape[1]
        lane = lax.broadcasted_iota(jnp.int32, (entries, COLS), 1)
        wanted = jnp.zeros((entries, COLS), jnp.int32)
        for b in range(4):
            wanted = jnp.where(lane // 32 == b, strips[b], wanted)
        entry = lax.broadcasted_iota(jnp.int32, (entries, COLS), 0)
        one_hot = jnp.where(entry == wanted, 1.0, 0.0).astype(jnp.bfloat16)
        lane_k = lax.broadcasted_iota(jnp.int32, (64, COLS), 1)

        def cell(c, total):
            rows = wts[pl.ds(pl.multiple_of(c * 64, 64), 64), :]
            mine = jnp.dot(rows, one_hot, preferred_element_type=jnp.float32)
            return jnp.where(lane_k % 32 == c, mine, total)
        total = lax.fori_loop(0, 32, cell, jnp.zeros((64, COLS), jnp.float32), unroll=4)
        for b in range(4):
            bd[64 * b:64 * b + 64, :] = jnp.where(lane_k // 32 == b, total, 0.0).astype(jnp.bfloat16)

    give_first_halo(sa)
    loads[4].wait()
    lax.fori_loop(0, LEVELS, pivots, 0, unroll=2)
    loads[5].wait()
    pick_weights()
    take_rows(0, sa)
    take_columns(0, (2, 3))
    lax.fori_loop(0, LEVELS, coefficients, 0, unroll=2)
    take_columns(0, (0, 1))
    for step in range(STEPS):
        state, new = (sa, sb) if step % 2 == 0 else (sb, sa)
        forward(state, new)
        backward(new)
        if step == STEPS - 1:
            store = pltpu.make_async_copy(new.at[:, pl.ds(PAD, ROWS), :], out_hbm, lsem.at[0])
            store.start()
        provide(step, new)
        route(step)
        if step == STEPS - 1:
            sort_and_send(step)
            hand_on(step)
        else:
            later = step + 1
            for group in range(3):
                pack_columns(later, new, group)
                send_columns(later, group)
            pl.when(jnp.logical_not(is_side))(lambda: give_rows(later, new))
            sort_and_send(step)
            take_columns(later, (0, 1, 2))
            pl.when(jnp.logical_not(is_side))(lambda: take_rows(later, new))
            fill(step, new)

            @pl.when(is_side)
            def _():
                give_rows(later, new)
            pl.when(is_band)(lambda: patch_columns(later, new))

            @pl.when(is_side)
            def _():
                take_rows(later, new)

    for step in range(STEPS):
        sent_halo(step)
        all_of(pay.at[step], p1s.at[step])

        @pl.when(is_mid)
        def _():
            all_of(ob.at[step, pl.ds(0, 4 * lon_n)], p2bs.at[step])
            all_of(ob.at[step, pl.ds(4 * lon_n, 2 * lat_n)], p2s.at[step])
    store.wait()


def last_fill(lat_n, lon_n, chunks, state, sides, bands, out, held, side, band, rsem, wsem, lsem):
    lat = lax.axis_index("lat")
    lon = lax.axis_index("lon")
    count = FIELDS // chunks
    is_side = (lon == 0) | (lon == lon_n - 1)
    is_band = (lat == 0) | (lat == lat_n - 1)
    start = jnp.where(lon == 0, 0, COLS - 2)
    lane = lax.broadcasted_iota(jnp.int32, (ROWS, COLS), 1)
    get_side = pltpu.make_async_copy(sides, side, lsem.at[0])
    get_band = pltpu.make_async_copy(bands, band, lsem.at[1])
    pl.when(is_side)(get_side.start)
    pl.when(is_band)(get_band.start)
    parts = [pl.ds(c * count, count) for c in range(chunks)]
    reads = [pltpu.make_async_copy(state.at[p], held.at[p], rsem.at[c]) for c, p in enumerate(parts)]
    writes = [pltpu.make_async_copy(held.at[p], out.at[p], wsem.at[c]) for c, p in enumerate(parts)]
    for read in reads:
        read.start()
    pl.when(is_side)(get_side.wait)
    pl.when(is_band)(get_band.wait)
    for c in range(chunks):
        reads[c].wait()
        fields = range(c * count, c * count + count)

        @pl.when(is_side)
        def _():
            for f in fields:
                a = pltpu.roll(side[f % 2], COLS - f, 1) if f else side[0]
                held[f] = jnp.where(lane // 2 == start // 2, a, held[f])

        for edge, row in ((0, 0), (lat_n - 1, ROWS - 2)):
            @pl.when(lat == edge)
            def _():
                for f in fields:
                    for r in range(2):
                        held[f, row + r:row + r + 1, :] = band[r, f:f + 1, :]

        writes[c].start()
    for write in writes:
        write.wait()


def on_device(lat_n, lon_n, tracers, winds, mixing, strip_source, strip_tile, weights):
    f32 = jnp.float32
    vm = pltpu.VMEM
    dma = pltpu.SemaphoreType.DMA
    devices = lat_n * lon_n
    tiles_out = 4 * lon_n + 2 * lat_n
    anywhere = pl.BlockSpec(memory_space=pl.ANY)
    smem = pl.BlockSpec(memory_space=pltpu.SMEM)
    in_vmem = pl.BlockSpec(memory_space=pltpu.VMEM)
    state, sides, bands = pl.pallas_call(
        functools.partial(kernel, lat_n, lon_n),
        out_shape=(
            jax.ShapeDtypeStruct((FIELDS, ROWS, COLS), f32),
            jax.ShapeDtypeStruct((2, ROWS, COLS), f32),
            jax.ShapeDtypeStruct((2, FIELDS, COLS), f32),
        ),
        in_specs=[smem, smem, in_vmem, anywhere, anywhere, anywhere, anywhere],
        out_specs=(anywhere, in_vmem, in_vmem),
        scratch_shapes=[
            vm((FIELDS, TALL, COLS), f32),
            vm((FIELDS, TALL, COLS), f32),
            vm((LEVELS, ROWS, COLS), f32),
            vm((LEVELS, TALL, COLS), f32),
            vm((LEVELS + 1, ROWS, COLS), f32),
            vm((LEVELS, 10, ROWS, COLS), f32),
            vm((LEVELS + 1, ROWS, COLS), f32),
            vm((LEVELS, ROWS, COLS), f32),
            vm((32 * 64, weights.shape[1]), weights.dtype),
            vm((256, COLS), jnp.bfloat16),
            vm((STEPS, 4, ROWS, COLS), f32),
            vm((STEPS, 2, 4, ROWS, COLS), f32),
            vm((3, 8, COLS), f32),
            vm((2, 3, 8, COLS), f32),
            vm((FIELDS + LEVELS, ROWS, COLS), f32),
            vm((STEPS, 2, FIELDS + LEVELS, 2, COLS), f32),
            vm((STEPS, 2, FIELDS + LEVELS, 2, COLS), f32),
            vm((2, ROWS, COLS), f32),
            vm((STEPS, MIDS, SHARE, COLS), f32),
            vm((devices, SHARE, COLS), f32),
            vm((devices, SHARE, COLS), f32),
            vm((strip_source.shape[1] // 16, 8, COLS), f32),
            vm((STEPS, tiles_out, SHARE, COLS), f32),
            vm((STEPS, MIDS, 2, SHARE, COLS), f32),
            vm((STEPS, MIDS, SHARE, COLS), f32),
            vm((2, 128, COLS), f32),
            vm((128, COLS), f32),
            dma((6,)),
            dma((STEPS, 4, 4)),
            dma((STEPS, 4, 4)),
            dma((2, 2)),
            dma((STEPS,)),
            dma((STEPS,)),
            dma((STEPS,)),
            dma((STEPS,)),
            dma((STEPS,)),
            dma((STEPS,)),
        ],
        compiler_params=pltpu.CompilerParams(
            collective_id=0, has_side_effects=True, vmem_limit_bytes=56 * 1024 * 1024),
    )(
        strip_source, strip_tile, strip_source,
        tracers.reshape(FIELDS, ROWS, COLS),
        winds.reshape(2, LEVELS, ROWS, COLS),
        mixing.reshape(LEVELS - 1, ROWS, COLS),
        jnp.transpose(weights, (0, 2, 3, 1)).reshape(2, 32 * 64, weights.shape[1]),
    )
    chunks = 6
    out = pl.pallas_call(
        functools.partial(last_fill, lat_n, lon_n, chunks),
        out_shape=jax.ShapeDtypeStruct((FIELDS, ROWS, COLS), f32),
        in_specs=[anywhere, anywhere, anywhere],
        out_specs=anywhere,
        scratch_shapes=[
            vm((FIELDS, ROWS, COLS), f32),
            vm((2, ROWS, COLS), f32),
            vm((2, FIELDS, COLS), f32),
            dma((chunks,)),
            dma((chunks,)),
            dma((2,)),
        ],
        compiler_params=pltpu.CompilerParams(vmem_limit_bytes=56 * 1024 * 1024),
    )(state, sides, bands)
    return out.reshape(tracers.shape)


def solution(mesh):
    return jax.shard_map(
        functools.partial(on_device, mesh.shape["lat"], mesh.shape["lon"]),
        mesh=mesh,
        in_specs=(
            P("panel", None, None, "lat", "lon"),
            P("panel", None, None, "lat", "lon"),
            P("panel", None, "lat", "lon"),
            P(),
            P(),
            P(),
        ),
        out_specs=P("panel", None, None, "lat", "lon"),
        check_vma=False,
    )
```

```python
import functools

import jax
import jax.numpy as jnp
from jax import lax
from jax.experimental import pallas as pl
from jax.experimental.pallas import tpu as pltpu
from jax.sharding import PartitionSpec as P

MESH = pl.DeviceIdType.MESH
STEPS = 2
MIDS = 9
FIELDS = 72
LEVELS = 36
ROWS = 64
COLS = 128
SHARE = FIELDS // MIDS
PAD = 8
TALL = ROWS + 2 * PAD
CHUNK = 16
EAST, WEST, SOUTH, NORTH = range(4)


def mid_place(k):
    j = k // 2
    return 1 + 5 * (k % 2), 4 * (j // 2) + 1 + j % 2 - 9 * (j // 8)


def kernel(lat_n, lon_n, ssrc, stile, vsrc, tr_hbm, wd_hbm, mix_hbm, wt_hbm,
           out_hbm, sides_out, bands_out,
           sa, sb, w0, w1, mx, cf, rt, iv, wts, bd, pk, pkr, pt, ptr, hb, rw, rwr, prev,
           pay, inb0, inb1, hs, ob, rb, rs, dense, flip,
           lsem, ssem, rsem, psem, p1s, p1r, p2s, p2bs, p2r, p2br):
    panel = lax.axis_index("panel")
    lat = lax.axis_index("lat")
    lon = lax.axis_index("lon")
    me = lat * lon_n + lon
    other = 1 - panel
    has = {
        EAST: lon < lon_n - 1,
        WEST: lon > 0,
        SOUTH: lat < lat_n - 1,
        NORTH: lat > 0,
    }
    beside = {
        EAST: (panel, lat, lon + 1),
        WEST: (panel, lat, lon - 1),
        SOUTH: (panel, lat + 1, lon),
        NORTH: (panel, lat - 1, lon),
    }
    is_band = (lat == 0) | (lat == lat_n - 1)
    is_side = (lon == 0) | (lon == lon_n - 1)
    mid_id = jnp.int32(-1)
    for k in range(MIDS):
        mlat, mlon = mid_place(k)
        mid_id = jnp.where((lat == mlat) & (lon == mlon), jnp.int32(k), mid_id)
    is_mid = mid_id >= 0
    inb = (inb0, inb1)
    lane8 = lax.broadcasted_iota(jnp.int32, (8, COLS), 1)
    lane_c = lax.broadcasted_iota(jnp.int32, (CHUNK, COLS), 1)

    early = 64
    loads = [
        pltpu.make_async_copy(wd_hbm.at[0], w0, lsem.at[0]),
        pltpu.make_async_copy(
            tr_hbm.at[pl.ds(early, FIELDS - early)],
            sa.at[pl.ds(early, FIELDS - early), pl.ds(PAD, ROWS), :], lsem.at[1]),
        pltpu.make_async_copy(
            tr_hbm.at[pl.ds(0, early)], sa.at[pl.ds(0, early), pl.ds(PAD, ROWS), :], lsem.at[2]),
        pltpu.make_async_copy(wd_hbm.at[1], w1.at[:, pl.ds(PAD, ROWS), :], lsem.at[3]),
        pltpu.make_async_copy(mix_hbm, mx.at[pl.ds(1, LEVELS - 1)], lsem.at[4]),
        pltpu.make_async_copy(wt_hbm.at[other], wts, lsem.at[5]),
    ]
    for load in loads[:4]:
        load.start()

    barrier = pltpu.get_barrier_semaphore()
    for way in range(4):
        @pl.when(has[way])
        def _():
            pl.semaphore_signal(barrier, inc=1, device_id=beside[way], device_id_type=MESH)

    @pl.when(is_mid)
    def _():
        def greet(i, carry):
            pl.semaphore_signal(
                barrier, inc=1, device_id=(other, i // lon_n, i % lon_n), device_id_type=MESH)
            return carry
        lax.fori_loop(0, lat_n * lon_n, greet, 0)

    def greet_mids():
        def greet(k, carry):
            mlat, mlon = mid_place(k)
            pl.semaphore_signal(
                barrier, inc=1, device_id=(panel, mlat, mlon), device_id_type=MESH)
            return carry
        lax.fori_loop(0, MIDS, greet, 0)

    pl.when(is_band)(greet_mids)
    pl.when(is_side)(greet_mids)
    one = jnp.int32(1)
    none = jnp.int32(0)
    expect = jnp.int32(MIDS)
    for way in range(4):
        expect = expect + jnp.where(has[way], one, none)
    expect = expect + jnp.where(is_mid, jnp.int32(2 * lon_n + 2 * lat_n), none)

    zero = jnp.zeros((ROWS, COLS), jnp.float32)
    mx[0] = zero
    mx[LEVELS] = zero
    rt[0] = zero
    for step in range(STEPS):
        for way in range(2):
            @pl.when(jnp.logical_not(has[way ^ 1]))
            def _():
                pkr[step, way] = jnp.zeros((4, ROWS, COLS), jnp.float32)

            @pl.when(jnp.logical_not(has[2 + (way ^ 1)]))
            def _():
                rwr[step, way] = jnp.zeros((FIELDS + LEVELS, 2, COLS), jnp.float32)
    for way in range(2):
        @pl.when(jnp.logical_not(has[way ^ 1]))
        def _():
            ptr[way] = jnp.zeros((3, 8, COLS), jnp.float32)

    loads[0].wait()
    loads[1].wait()
    loads[4].start()
    loads[5].start()

    def fields_of(step):
        return FIELDS + LEVELS if step == 0 else FIELDS

    def groups_of(step):
        return (fields_of(step) + 31) // 32

    def rows_copy(step, way):
        part = pl.ds(0, fields_of(step))
        return pltpu.make_async_remote_copy(
            src_ref=rw.at[step, way - 2, part], dst_ref=rwr.at[step, way - 2, part],
            send_sem=ssem.at[step, way, 0], recv_sem=rsem.at[step, way, 0],
            device_id=beside[way], device_id_type=MESH)

    def columns_copy(step, way, group):
        return pltpu.make_async_remote_copy(
            src_ref=pk.at[step, group], dst_ref=pkr.at[step, way, group],
            send_sem=ssem.at[step, way, group], recv_sem=rsem.at[step, way, group],
            device_id=beside[way], device_id_type=MESH)

    def send_columns(step, group):
        for way in (EAST, WEST):
            @pl.when(has[way])
            def _():
                columns_copy(step, way, group).start()

    def packed(step, state, group, g):
        rows = pl.ds(pl.multiple_of(PAD + g * 8, 8), 8)
        bare = pl.ds(pl.multiple_of(g * 8, 8), 8)
        total = jnp.zeros((8, COLS), jnp.float32)
        for slot in range(min(32, fields_of(step) - 32 * group)):
            f = 32 * group + slot
            value = state[f, rows, :] if f < FIELDS else w0[f - FIELDS, bare, :]
            moved = pltpu.roll(value, (4 * slot + 2) % COLS, 1)
            total = jnp.where(lane8 // 4 == slot, moved, total)
        return total

    def unpacked(step, group, g, from_west, from_east):
        both = jnp.where(lane8 % 4 < 2, from_west, from_east)
        rows = pl.ds(pl.multiple_of(g * 8, 8), 8)
        for slot in range(min(32, fields_of(step) - 32 * group)):
            hb[32 * group + slot, rows, :] = pltpu.roll(both, (2 * COLS - 2 - 4 * slot) % COLS, 1)

    def pack_columns(step, state, group):
        def pack(g, carry):
            pk[step, group, pl.ds(pl.multiple_of(g * 8, 8), 8), :] = packed(step, state, group, g)
            return carry
        lax.fori_loop(0, ROWS // 8, pack, 0, unroll=2)

    def give_rows(step, state):
        def rows_of(f, carry):
            rw[step, 0, f] = state[f, PAD + ROWS - 2:PAD + ROWS, :]
            rw[step, 1, f] = state[f, PAD:PAD + 2, :]
            return carry
        lax.fori_loop(0, FIELDS, rows_of, 0, unroll=8)
        if step == 0:
            def winds_of(l, carry):
                rw[step, 0, FIELDS + l] = w1[l, PAD + ROWS - 2:PAD + ROWS, :]
                rw[step, 1, FIELDS + l] = w1[l, PAD:PAD + 2, :]
                return carry
            lax.fori_loop(0, LEVELS, winds_of, 0, unroll=4)
        for way in (SOUTH, NORTH):
            @pl.when(has[way])
            def _():
                rows_copy(step, way).start()

    def give_first_halo(state):
        pack_columns(0, state, 2)
        pl.semaphore_wait(barrier, expect)
        send_columns(0, 2)
        pack_columns(0, state, 3)
        send_columns(0, 3)
        loads[2].wait()
        loads[3].wait()
        give_rows(0, state)
        for group in range(2):
            pack_columns(0, state, group)
            send_columns(0, group)

    def take_rows(step, state):
        for way, came in ((SOUTH, NORTH), (NORTH, SOUTH)):
            @pl.when(has[came])
            def _():
                rows_copy(step, way).wait_recv()

        def rows_of(f, carry):
            state[f, PAD - 2:PAD, :] = rwr[step, 0, f]
            state[f, PAD + ROWS:PAD + ROWS + 2, :] = rwr[step, 1, f]
            return carry
        lax.fori_loop(0, FIELDS, rows_of, 0, unroll=8)
        if step == 0:
            def winds_of(l, carry):
                w1[l, PAD - 2:PAD, :] = rwr[step, 0, FIELDS + l]
                w1[l, PAD + ROWS:PAD + ROWS + 2, :] = rwr[step, 1, FIELDS + l]
                return carry
            lax.fori_loop(0, LEVELS, winds_of, 0, unroll=4)
    def take_columns(step, groups):
        for group in groups:
            for way, came in ((EAST, WEST), (WEST, EAST)):
                @pl.when(has[came])
                def _():
                    columns_copy(step, way, group).wait_recv()

            def unpack(g, carry):
                rows = pl.ds(pl.multiple_of(g * 8, 8), 8)
                unpacked(step, group, g, pkr[step, EAST, group, rows, :], pkr[step, WEST, group, rows, :])
                return carry
            lax.fori_loop(0, ROWS // 8, unpack, 0, unroll=2)

    def patch_copy(way):
        return pltpu.make_async_remote_copy(
            src_ref=pt, dst_ref=ptr.at[way], send_sem=psem.at[0, way], recv_sem=psem.at[1, way],
            device_id=beside[way], device_id_type=MESH)

    def patch_columns(step, state):
        for edge, g in ((0, 0), (lat_n - 1, ROWS // 8 - 1)):
            @pl.when(lat == edge)
            def _():
                for group in range(3):
                    pt[group] = packed(step, state, group, g)
        for way in (EAST, WEST):
            @pl.when(has[way])
            def _():
                patch_copy(way).start()

    def take_patch(step):
        for way in (EAST, WEST):
            @pl.when(has[way ^ 1])
            def _():
                patch_copy(way).wait_recv()
        for edge, g in ((0, 0), (lat_n - 1, ROWS // 8 - 1)):
            @pl.when(lat == edge)
            def _():
                for group in range(3):
                    unpacked(step, group, g, ptr[EAST, group], ptr[WEST, group])

    def sent_halo(step):
        for way in range(4):
            @pl.when(has[way])
            def _():
                if way in (EAST, WEST):
                    for group in range(groups_of(step)):
                        columns_copy(step, way, group).wait_send()
                    if step > 0:
                        pl.when(is_band)(patch_copy(way).wait_send)
                else:
                    rows_copy(step, way).wait_send()

    def pivots(l, carry):
        for g in range(ROWS // CHUNK):
            rows = pl.ds(g * CHUNK, CHUNK)
            low = mx[l, rows, :]
            high = mx[l + 1, rows, :]
            inv = 1.0 / (1.0 + low + high - low * rt[l, rows, :])
            iv[l, rows, :] = inv
            rt[l + 1, rows, :] = high * inv
            cf[l, 9, rows, :] = low * inv
        return carry

    def coefficients(l, carry):
        for g in range(ROWS // CHUNK):
            rows = pl.ds(g * CHUNK, CHUNK)
            w = w0[l, rows, :]
            beyond = hb[FIELDS + l, rows, :]
            w_east = pltpu.roll(jnp.where(lane_c < 1, beyond, w), COLS - 1, 1)
            w_west = pltpu.roll(jnp.where(lane_c >= COLS - 1, beyond, w), 1, 1)
            base = PAD + g * CHUNK
            v = w1[l, base:base + CHUNK, :]
            v_next = w1[l, base + 1:base + CHUNK + 1, :]
            v_prev = w1[l, base - 1:base + CHUNK - 1, :]

            def parts(face):
                face = face * (1.0 / 12.0)
                return jnp.maximum(face, 0.0), jnp.minimum(face, 0.0)

            pe, me_ = parts(w + w_east)
            pw, mw = parts(w + w_west)
            pn, mn = parts(v + v_next)
            ps, ms = parts(v + v_prev)
            inv = iv[l, rows, :]
            centre = 1.0 + (2.0 * (pw - me_) + 5.0 * (mw - pe)) + (2.0 * (ps - mn) + 5.0 * (ms - pn))
            for i, c in enumerate((
                centre,
                -pw, 5.0 * pw + 2.0 * mw + pe, -mw - 2.0 * pe - 5.0 * me_, me_,
                -ps, 5.0 * ps + 2.0 * ms + pn, -ms - 2.0 * pn - 5.0 * mn, mn,
            )):
                cf[l, i, rows, :] = c * inv
        return carry

    def forward(state, new, chunks):
        for g in chunks:
            prev[:, g * CHUNK:g * CHUNK + CHUNK, :] = jnp.zeros((2, CHUNK, COLS), jnp.float32)

        def level(l, carry):
            for g in chunks:
                rows = pl.ds(g * CHUNK, CHUNK)
                base = PAD + g * CHUNK
                for t in range(2):
                    f = t * LEVELS + l
                    q = state[f, base:base + CHUNK, :]
                    beyond = hb[f, rows, :]
                    x = cf[l, 0, rows, :] * q
                    x += cf[l, 1, rows, :] * pltpu.roll(jnp.where(lane_c >= COLS - 2, beyond, q), 2, 1)
                    x += cf[l, 2, rows, :] * pltpu.roll(jnp.where(lane_c >= COLS - 1, beyond, q), 1, 1)
                    x += cf[l, 3, rows, :] * pltpu.roll(jnp.where(lane_c < 1, beyond, q), COLS - 1, 1)
                    x += cf[l, 4, rows, :] * pltpu.roll(jnp.where(lane_c < 2, beyond, q), COLS - 2, 1)
                    x += cf[l, 5, rows, :] * state[f, base - 2:base - 2 + CHUNK, :]
                    x += cf[l, 6, rows, :] * state[f, base - 1:base - 1 + CHUNK, :]
                    x += cf[l, 7, rows, :] * state[f, base + 1:base + 1 + CHUNK, :]
                    x += cf[l, 8, rows, :] * state[f, base + 2:base + 2 + CHUNK, :]
                    x += cf[l, 9, rows, :] * prev[t, rows, :]
                    prev[t, rows, :] = x
                    new[f, base:base + CHUNK, :] = x
            return carry
        lax.fori_loop(0, LEVELS, level, 0, unroll=8 // len(chunks))

    def backward(new, chunks):
        def level(i, carry):
            l = LEVELS - 2 - i
            for g in chunks:
                rows = pl.ds(g * CHUNK, CHUNK)
                base = PAD + g * CHUNK
                for t in range(2):
                    f = t * LEVELS + l
                    x = new[f, base:base + CHUNK, :] + rt[l + 1, rows, :] * prev[t, rows, :]
                    prev[t, rows, :] = x
                    new[f, base:base + CHUNK, :] = x
            return carry
        lax.fori_loop(0, LEVELS - 1, level, 0, unroll=5)

    def to_mid(step, k):
        mlat, mlon = mid_place(k)
        return pltpu.make_async_remote_copy(
            src_ref=pay.at[step, k], dst_ref=inb[step].at[me], send_sem=p1s.at[step],
            recv_sem=p1r.at[step], device_id=(other, mlat, mlon), device_id_type=MESH)

    def to_band(step, d):
        return pltpu.make_async_remote_copy(
            src_ref=ob.at[step, pl.ds(2 * d, 2)], dst_ref=rb.at[step, mid_id],
            send_sem=p2bs.at[step], recv_sem=p2br.at[step],
            device_id=(panel, (d // lon_n) * (lat_n - 1), d % lon_n), device_id_type=MESH)

    def to_side(step, e):
        return pltpu.make_async_remote_copy(
            src_ref=ob.at[step, 4 * lon_n + e], dst_ref=rs.at[step, mid_id],
            send_sem=p2s.at[step], recv_sem=p2r.at[step],
            device_id=(panel, e % lat_n, (e // lat_n) * (lon_n - 1)), device_id_type=MESH)

    def all_of(ref, sem):
        pltpu.make_async_copy(ref, ref, sem).wait()

    def provide(step, new, tiles):
        flat = new.reshape(FIELDS * TALL, COLS)
        lane_f = lax.broadcasted_iota(jnp.int32, (FIELDS, COLS), 1)
        total = jnp.zeros((FIELDS, COLS), jnp.float32)
        for pair in range(2):
            cells = jnp.zeros((FIELDS, COLS), jnp.float32)
            for s in range(2):
                tile = tiles[2 * pair + s]
                first = PAD + (tile // 8) * 4
                for r in range(4):
                    row = flat[pl.ds(first + r, FIELDS, stride=TALL), :]
                    shift = (2 * COLS + 64 * s + 16 * r - 16 * (tile % 8)) % COLS
                    row = pltpu.roll(row, shift, 1)
                    cells = jnp.where(lane_f // 16 == 4 * s + r, row, cells)
            w = bd[128 * pair:128 * pair + 128, :]
            rest = cells
            for part in range(3):
                piece = rest.astype(jnp.bfloat16)
                total += jnp.dot(piece, w, preferred_element_type=jnp.float32)
                if part < 2:
                    rest = rest - piece.astype(jnp.float32)
        pay[step] = total.reshape(MIDS, SHARE, COLS)

    def route(step):
        def send(k, carry):
            to_mid(step, k).start()
            return carry
        lax.fori_loop(0, MIDS, send, 0)

    def sort_and_send(step):
        @pl.when(is_mid)
        def _():
            if step == 0:
                pairs = ssrc.shape[1] // 2
                shape = (pairs, 2 * pairs)
                row = jnp.where(panel == 0, vsrc[0:1, :], vsrc[1:2, :]).astype(jnp.float32)
                row = jnp.broadcast_to(row, shape)
                lane = lax.broadcasted_iota(jnp.int32, shape, 1)
                pair = lax.broadcasted_iota(jnp.int32, shape, 0)
                own = jnp.sum(jnp.where(lane == 2 * pair, row, 0.0), axis=1, keepdims=True)
                same = (row == own) & (lane % 2 == 0) & (lane < 2 * pair)
                second = jnp.max(jnp.where(same, 1.0, 0.0), axis=1, keepdims=True)
                hs[...] = jnp.broadcast_to(second, (pairs, COLS)).reshape(pairs // 8, 8, COLS)
            all_of(inb[step], p1r.at[step])
            lane_s = lax.broadcasted_iota(jnp.int32, (SHARE, COLS), 1)
            batch = 8

            def sort(i):
                done = []
                for j in range(batch):
                    u = i * batch + j
                    a = inb[step][ssrc[panel, 4 * u]]
                    b = inb[step][ssrc[panel, 4 * u + 2]]
                    line = hs[2 * i + j // 4]
                    second_a = line[2 * j % 8:2 * j % 8 + 1, :] > 0.5
                    second_b = line[2 * j % 8 + 1:2 * j % 8 + 2, :] > 0.5
                    a = jnp.where(second_a, pltpu.roll(a, 64, 1), a)
                    b = jnp.where(second_b, b, pltpu.roll(b, 64, 1))
                    done.append(jnp.where(lane_s < 64, a, b))
                for j in range(batch):
                    ob[step, i * batch + j] = done[j]

            def sides(i, carry):
                sort(4 * lon_n // batch + i)
                for j in range(batch):
                    to_side(step, batch * i + j).start()
                return carry
            lax.fori_loop(0, 2 * lat_n // batch, sides, 0)

            def bands(i, carry):
                sort(i)
                for j in range(batch // 2):
                    to_band(step, batch // 2 * i + j).start()
                return carry
            lax.fori_loop(0, 4 * lon_n // batch, bands, 0)

    def side_lines(step):
        all_of(rs.at[step], p2r.at[step])
        dense[0, 0:FIELDS, :] = rs[step].reshape(FIELDS, COLS)
        flip[...] = jnp.transpose(dense[0])
        first = flip[pl.ds(0, ROWS, stride=2), :]
        second = pltpu.roll(flip[pl.ds(1, ROWS, stride=2), :], 1, 1)
        even = lax.broadcasted_iota(jnp.int32, (ROWS, COLS), 1) % 2 == 0
        start = jnp.where(lon == 0, 0, COLS - 2)
        return (pltpu.roll(jnp.where(even, first, second), start, 1),
                pltpu.roll(jnp.where(even, second, first), start, 1))

    def band_lines(step):
        all_of(rb.at[step], p2br.at[step])
        lane_f = lax.broadcasted_iota(jnp.int32, (FIELDS, COLS), 1)
        lines = []
        for r in range(2):
            line = jnp.zeros((FIELDS, COLS), jnp.float32)
            for u in range(2):
                tiles = rb[step, :, u].reshape(FIELDS, COLS)
                for s in range(4):
                    moved = pltpu.roll(tiles, (2 * COLS + 64 * u - 16 * s - 16 * r) % COLS, 1)
                    line = jnp.where(lane_f // 16 == 4 * u + s, moved, line)
            lines.append(line)
        return lines

    def fill(step, new):
        @pl.when(is_side)
        def _():
            dense[0, 0:ROWS, :], dense[1, 0:ROWS, :] = side_lines(step)
            start = jnp.where(lon == 0, 0, COLS - 2)

            def column(g, carry):
                rows = pl.ds(pl.multiple_of(PAD + g * 8, 8), 8)
                bare = pl.ds(pl.multiple_of(g * 8, 8), 8)
                pair = dense[0, bare, :], dense[1, bare, :]
                for f in range(FIELDS):
                    a = pltpu.roll(pair[f % 2], COLS - f, 1) if f else pair[0]
                    new[f, rows, :] = jnp.where(lane8 // 2 == start // 2, a, new[f, rows, :])
                return carry
            lax.fori_loop(0, ROWS // 8, column, 0)

        @pl.when(is_band)
        def _():
            lines = band_lines(step)
            flat = new.reshape(FIELDS * TALL, COLS)
            for r in range(2):
                @pl.when(lat == 0)
                def _():
                    flat[pl.ds(PAD + r, FIELDS, stride=TALL), :] = lines[r]

                @pl.when(lat == lat_n - 1)
                def _():
                    flat[pl.ds(PAD + ROWS - 2 + r, FIELDS, stride=TALL), :] = lines[r]

    def hand_on(step):
        @pl.when(is_side)
        def _():
            sides_out[0], sides_out[1] = side_lines(step)

        @pl.when(is_band)
        def _():
            bands_out[0], bands_out[1] = band_lines(step)

    def pick_weights(strips):
        entries = wts.shape[1]
        lane = lax.broadcasted_iota(jnp.int32, (entries, COLS), 1)
        wanted = jnp.zeros((entries, COLS), jnp.int32)
        for b in range(4):
            wanted = jnp.where(lane // 32 == b, strips[b], wanted)
        entry = lax.broadcasted_iota(jnp.int32, (entries, COLS), 0)
        one_hot = jnp.where(entry == wanted, 1.0, 0.0).astype(jnp.bfloat16)
        lane_k = lax.broadcasted_iota(jnp.int32, (64, COLS), 1)

        def cell(c, total):
            rows = wts[pl.ds(pl.multiple_of(c * 64, 64), 64), :]
            mine = jnp.dot(rows, one_hot, preferred_element_type=jnp.float32)
            return jnp.where(lane_k % 32 == c, mine, total)
        total = lax.fori_loop(0, 32, cell, jnp.zeros((64, COLS), jnp.float32), unroll=4)
        for b in range(4):
            bd[64 * b:64 * b + 64, :] = jnp.where(lane_k // 32 == b, total, 0.0).astype(jnp.bfloat16)

    give_first_halo(sa)

    def look(i, found):
        first, second = found
        for j in range(8):
            m = 8 * i + j
            hit = ssrc[other, 2 * m] == me
            second = jnp.where(hit & (first >= 0), m, second)
            first = jnp.where(hit & (first < 0), m, first)
        return first, second
    found = lax.fori_loop(0, ssrc.shape[1] // 16, look, (jnp.int32(-1), jnp.int32(-1)))
    found = [jnp.maximum(m, 0) for m in found]
    strips = [2 * m + s for m in found for s in range(2)]
    tiles = [stile[other, strip] for strip in strips]

    loads[4].wait()
    lax.fori_loop(0, LEVELS, pivots, 0, unroll=2)
    loads[5].wait()
    pick_weights(strips)
    take_rows(0, sa)
    take_columns(0, (2, 3))
    lax.fori_loop(0, LEVELS, coefficients, 0, unroll=2)
    take_columns(0, (0, 1))
    for step in range(STEPS):
        state, new = (sa, sb) if step % 2 == 0 else (sb, sa)
        if step == 0:
            inner, outer = (), tuple(range(ROWS // CHUNK))
        else:
            inner, outer = tuple(range(1, ROWS // CHUNK - 1)), (0, ROWS // CHUNK - 1)
            forward(state, new, inner)
            backward(new, inner)
            pl.when(is_band)(lambda: take_patch(step))

            @pl.when(is_side)
            def _():
                take_rows(step, state)
        forward(state, new, outer)
        backward(new, outer)
        if step == STEPS - 1:
            store = pltpu.make_async_copy(new.at[:, pl.ds(PAD, ROWS), :], out_hbm, lsem.at[0])
            store.start()
        provide(step, new, tiles)
        route(step)
        if step == STEPS - 1:
            sort_and_send(step)
            hand_on(step)
        else:
            later = step + 1
            for group in range(3):
                pack_columns(later, new, group)
                send_columns(later, group)
            pl.when(jnp.logical_not(is_side))(lambda: give_rows(later, new))
            sort_and_send(step)
            take_columns(later, (0, 1, 2))
            pl.when(jnp.logical_not(is_side))(lambda: take_rows(later, new))
            fill(step, new)

            @pl.when(is_side)
            def _():
                give_rows(later, new)
            pl.when(is_band)(lambda: patch_columns(later, new))

    for step in range(STEPS):
        sent_halo(step)
        all_of(pay.at[step], p1s.at[step])

        @pl.when(is_mid)
        def _():
            all_of(ob.at[step, pl.ds(0, 4 * lon_n)], p2bs.at[step])
            all_of(ob.at[step, pl.ds(4 * lon_n, 2 * lat_n)], p2s.at[step])
    store.wait()


def last_fill(lat_n, lon_n, chunks, state, sides, bands, out, held, side, band, rsem, wsem, lsem):
    lat = lax.axis_index("lat")
    lon = lax.axis_index("lon")
    count = FIELDS // chunks
    is_side = (lon == 0) | (lon == lon_n - 1)
    is_band = (lat == 0) | (lat == lat_n - 1)
    start = jnp.where(lon == 0, 0, COLS - 2)
    lane = lax.broadcasted_iota(jnp.int32, (ROWS, COLS), 1)
    get_side = pltpu.make_async_copy(sides, side, lsem.at[0])
    get_band = pltpu.make_async_copy(bands, band, lsem.at[1])
    pl.when(is_side)(get_side.start)
    pl.when(is_band)(get_band.start)
    parts = [pl.ds(c * count, count) for c in range(chunks)]
    reads = [pltpu.make_async_copy(state.at[p], held.at[p], rsem.at[c]) for c, p in enumerate(parts)]
    writes = [pltpu.make_async_copy(held.at[p], out.at[p], wsem.at[c]) for c, p in enumerate(parts)]
    for read in reads:
        read.start()
    pl.when(is_side)(get_side.wait)
    pl.when(is_band)(get_band.wait)
    for c in range(chunks):
        reads[c].wait()
        fields = range(c * count, c * count + count)

        @pl.when(is_side)
        def _():
            for f in fields:
                a = pltpu.roll(side[f % 2], COLS - f, 1) if f else side[0]
                held[f] = jnp.where(lane // 2 == start // 2, a, held[f])

        for edge, row in ((0, 0), (lat_n - 1, ROWS - 2)):
            @pl.when(lat == edge)
            def _():
                for f in fields:
                    for r in range(2):
                        held[f, row + r:row + r + 1, :] = band[r, f:f + 1, :]

        writes[c].start()
    for write in writes:
        write.wait()


def on_device(lat_n, lon_n, tracers, winds, mixing, strip_source, strip_tile, weights):
    f32 = jnp.float32
    vm = pltpu.VMEM
    dma = pltpu.SemaphoreType.DMA
    devices = lat_n * lon_n
    tiles_out = 4 * lon_n + 2 * lat_n
    anywhere = pl.BlockSpec(memory_space=pl.ANY)
    smem = pl.BlockSpec(memory_space=pltpu.SMEM)
    in_vmem = pl.BlockSpec(memory_space=pltpu.VMEM)
    state, sides, bands = pl.pallas_call(
        functools.partial(kernel, lat_n, lon_n),
        out_shape=(
            jax.ShapeDtypeStruct((FIELDS, ROWS, COLS), f32),
            jax.ShapeDtypeStruct((2, ROWS, COLS), f32),
            jax.ShapeDtypeStruct((2, FIELDS, COLS), f32),
        ),
        in_specs=[smem, smem, in_vmem, anywhere, anywhere, anywhere, anywhere],
        out_specs=(anywhere, in_vmem, in_vmem),
        scratch_shapes=[
            vm((FIELDS, TALL, COLS), f32),
            vm((FIELDS, TALL, COLS), f32),
            vm((LEVELS, ROWS, COLS), f32),
            vm((LEVELS, TALL, COLS), f32),
            vm((LEVELS + 1, ROWS, COLS), f32),
            vm((LEVELS, 10, ROWS, COLS), f32),
            vm((LEVELS + 1, ROWS, COLS), f32),
            vm((LEVELS, ROWS, COLS), f32),
            vm((32 * 64, weights.shape[1]), weights.dtype),
            vm((256, COLS), jnp.bfloat16),
            vm((STEPS, 4, ROWS, COLS), f32),
            vm((STEPS, 2, 4, ROWS, COLS), f32),
            vm((3, 8, COLS), f32),
            vm((2, 3, 8, COLS), f32),
            vm((FIELDS + LEVELS, ROWS, COLS), f32),
            vm((STEPS, 2, FIELDS + LEVELS, 2, COLS), f32),
            vm((STEPS, 2, FIELDS + LEVELS, 2, COLS), f32),
            vm((2, ROWS, COLS), f32),
            vm((STEPS, MIDS, SHARE, COLS), f32),
            vm((devices, SHARE, COLS), f32),
            vm((devices, SHARE, COLS), f32),
            vm((strip_source.shape[1] // 16, 8, COLS), f32),
            vm((STEPS, tiles_out, SHARE, COLS), f32),
            vm((STEPS, MIDS, 2, SHARE, COLS), f32),
            vm((STEPS, MIDS, SHARE, COLS), f32),
            vm((2, 128, COLS), f32),
            vm((128, COLS), f32),
            dma((6,)),
            dma((STEPS, 4, 4)),
            dma((STEPS, 4, 4)),
            dma((2, 2)),
            dma((STEPS,)),
            dma((STEPS,)),
            dma((STEPS,)),
            dma((STEPS,)),
            dma((STEPS,)),
            dma((STEPS,)),
        ],
        compiler_params=pltpu.CompilerParams(
            collective_id=0, has_side_effects=True, vmem_limit_bytes=56 * 1024 * 1024),
    )(
        strip_source, strip_tile, strip_source,
        tracers.reshape(FIELDS, ROWS, COLS),
        winds.reshape(2, LEVELS, ROWS, COLS),
        mixing.reshape(LEVELS - 1, ROWS, COLS),
        jnp.transpose(weights, (0, 2, 3, 1)).reshape(2, 32 * 64, weights.shape[1]),
    )
    chunks = 6
    out = pl.pallas_call(
        functools.partial(last_fill, lat_n, lon_n, chunks),
        out_shape=jax.ShapeDtypeStruct((FIELDS, ROWS, COLS), f32),
        in_specs=[anywhere, anywhere, anywhere],
        out_specs=anywhere,
        scratch_shapes=[
            vm((FIELDS, ROWS, COLS), f32),
            vm((2, ROWS, COLS), f32),
            vm((2, FIELDS, COLS), f32),
            dma((chunks,)),
            dma((chunks,)),
            dma((2,)),
        ],
        compiler_params=pltpu.CompilerParams(vmem_limit_bytes=56 * 1024 * 1024),
    )(state, sides, bands)
    return out.reshape(tracers.shape)


def solution(mesh):
    return jax.shard_map(
        functools.partial(on_device, mesh.shape["lat"], mesh.shape["lon"]),
        mesh=mesh,
        in_specs=(
            P("panel", None, None, "lat", "lon"),
            P("panel", None, None, "lat", "lon"),
            P("panel", None, "lat", "lon"),
            P(),
            P(),
            P(),
        ),
        out_specs=P("panel", None, None, "lat", "lon"),
        check_vma=False,
    )
```

```python
import functools

import jax
import jax.numpy as jnp
from jax import lax
from jax.experimental import pallas as pl
from jax.experimental.pallas import tpu as pltpu
from jax.sharding import PartitionSpec as P

MESH = pl.DeviceIdType.MESH
STEPS = 2
MIDS = 9
FIELDS = 72
LEVELS = 36
ROWS = 64
COLS = 128
SHARE = FIELDS // MIDS
PAD = 8
TALL = ROWS + 2 * PAD
CHUNK = 16
EAST, WEST, SOUTH, NORTH = range(4)


def mid_place(k):
    j = k // 2
    return 1 + 5 * (k % 2), 4 * (j // 2) + 1 + j % 2 - 9 * (j // 8)


def kernel(lat_n, lon_n, ssrc, stile, vsrc, tr_hbm, wd_hbm, mix_hbm, wt_hbm,
           out_hbm, sides_out, bands_out,
           sa, sb, w0, w1, mx, cf, rt, iv, wts, bd, pk, pkr, pt, ptr, hb, rw, rwr, prev,
           pay, inb0, inb1, hs, ob, rb, rs, dense, flip,
           lsem, ssem, rsem, psem, p1s, p1r, p2s, p2bs, p2r, p2br):
    panel = lax.axis_index("panel")
    lat = lax.axis_index("lat")
    lon = lax.axis_index("lon")
    me = lat * lon_n + lon
    other = 1 - panel
    has = {
        EAST: lon < lon_n - 1,
        WEST: lon > 0,
        SOUTH: lat < lat_n - 1,
        NORTH: lat > 0,
    }
    beside = {
        EAST: (panel, lat, lon + 1),
        WEST: (panel, lat, lon - 1),
        SOUTH: (panel, lat + 1, lon),
        NORTH: (panel, lat - 1, lon),
    }
    is_band = (lat == 0) | (lat == lat_n - 1)
    is_side = (lon == 0) | (lon == lon_n - 1)
    mid_id = jnp.int32(-1)
    for k in range(MIDS):
        mlat, mlon = mid_place(k)
        mid_id = jnp.where((lat == mlat) & (lon == mlon), jnp.int32(k), mid_id)
    is_mid = mid_id >= 0
    inb = (inb0, inb1)
    lane8 = lax.broadcasted_iota(jnp.int32, (8, COLS), 1)
    lane_c = lax.broadcasted_iota(jnp.int32, (CHUNK, COLS), 1)

    early = 64
    loads = [
        pltpu.make_async_copy(wd_hbm.at[0], w0, lsem.at[0]),
        pltpu.make_async_copy(
            tr_hbm.at[pl.ds(early, FIELDS - early)],
            sa.at[pl.ds(early, FIELDS - early), pl.ds(PAD, ROWS), :], lsem.at[1]),
        pltpu.make_async_copy(
            tr_hbm.at[pl.ds(0, early)], sa.at[pl.ds(0, early), pl.ds(PAD, ROWS), :], lsem.at[2]),
        pltpu.make_async_copy(wd_hbm.at[1], w1.at[:, pl.ds(PAD, ROWS), :], lsem.at[3]),
        pltpu.make_async_copy(mix_hbm, mx.at[pl.ds(1, LEVELS - 1)], lsem.at[4]),
        pltpu.make_async_copy(wt_hbm.at[other], wts, lsem.at[5]),
    ]
    for load in loads[:4]:
        load.start()

    barrier = pltpu.get_barrier_semaphore()
    for way in range(4):
        @pl.when(has[way])
        def _():
            pl.semaphore_signal(barrier, inc=1, device_id=beside[way], device_id_type=MESH)

    @pl.when(is_mid)
    def _():
        def greet(i, carry):
            pl.semaphore_signal(
                barrier, inc=1, device_id=(other, i // lon_n, i % lon_n), device_id_type=MESH)
            return carry
        lax.fori_loop(0, lat_n * lon_n, greet, 0)

    def greet_mids():
        def greet(k, carry):
            mlat, mlon = mid_place(k)
            pl.semaphore_signal(
                barrier, inc=1, device_id=(panel, mlat, mlon), device_id_type=MESH)
            return carry
        lax.fori_loop(0, MIDS, greet, 0)

    pl.when(is_band)(greet_mids)
    pl.when(is_side)(greet_mids)
    one = jnp.int32(1)
    none = jnp.int32(0)
    expect = jnp.int32(MIDS)
    for way in range(4):
        expect = expect + jnp.where(has[way], one, none)
    expect = expect + jnp.where(is_mid, jnp.int32(2 * lon_n + 2 * lat_n), none)

    zero = jnp.zeros((ROWS, COLS), jnp.float32)
    mx[0] = zero
    mx[LEVELS] = zero
    rt[0] = zero
    for step in range(STEPS):
        for way in range(2):
            @pl.when(jnp.logical_not(has[way ^ 1]))
            def _():
                pkr[step, way] = jnp.zeros((4, ROWS, COLS), jnp.float32)

            @pl.when(jnp.logical_not(has[2 + (way ^ 1)]))
            def _():
                rwr[step, way] = jnp.zeros((FIELDS + LEVELS, 2, COLS), jnp.float32)
    for way in range(2):
        @pl.when(jnp.logical_not(has[way ^ 1]))
        def _():
            ptr[way] = jnp.zeros((3, 8, COLS), jnp.float32)

    loads[0].wait()
    loads[1].wait()
    loads[4].start()
    loads[5].start()

    def fields_of(step):
        return FIELDS + LEVELS if step == 0 else FIELDS

    def groups_of(step):
        return (fields_of(step) + 31) // 32

    def rows_copy(step, way):
        part = pl.ds(0, fields_of(step))
        return pltpu.make_async_remote_copy(
            src_ref=rw.at[step, way - 2, part], dst_ref=rwr.at[step, way - 2, part],
            send_sem=ssem.at[step, way, 0], recv_sem=rsem.at[step, way, 0],
            device_id=beside[way], device_id_type=MESH)

    def columns_copy(step, way, group):
        return pltpu.make_async_remote_copy(
            src_ref=pk.at[step, group], dst_ref=pkr.at[step, way, group],
            send_sem=ssem.at[step, way, group], recv_sem=rsem.at[step, way, group],
            device_id=beside[way], device_id_type=MESH)

    def send_columns(step, group):
        for way in (EAST, WEST):
            @pl.when(has[way])
            def _():
                columns_copy(step, way, group).start()

    def packed(step, state, group, g):
        rows = pl.ds(pl.multiple_of(PAD + g * 8, 8), 8)
        bare = pl.ds(pl.multiple_of(g * 8, 8), 8)
        total = jnp.zeros((8, COLS), jnp.float32)
        for slot in range(min(32, fields_of(step) - 32 * group)):
            f = 32 * group + slot
            value = state[f, rows, :] if f < FIELDS else w0[f - FIELDS, bare, :]
            moved = pltpu.roll(value, (4 * slot + 2) % COLS, 1)
            total = jnp.where(lane8 // 4 == slot, moved, total)
        return total

    def unpacked(step, group, g, from_west, from_east):
        both = jnp.where(lane8 % 4 < 2, from_west, from_east)
        rows = pl.ds(pl.multiple_of(g * 8, 8), 8)
        for slot in range(min(32, fields_of(step) - 32 * group)):
            hb[32 * group + slot, rows, :] = pltpu.roll(both, (2 * COLS - 2 - 4 * slot) % COLS, 1)

    def pack_columns(step, state, group):
        def pack(g, carry):
            pk[step, group, pl.ds(pl.multiple_of(g * 8, 8), 8), :] = packed(step, state, group, g)
            return carry
        lax.fori_loop(0, ROWS // 8, pack, 0, unroll=2)

    def give_rows(step, state):
        def rows_of(f, carry):
            rw[step, 0, f] = state[f, PAD + ROWS - 2:PAD + ROWS, :]
            rw[step, 1, f] = state[f, PAD:PAD + 2, :]
            return carry
        lax.fori_loop(0, FIELDS, rows_of, 0, unroll=8)
        if step == 0:
            def winds_of(l, carry):
                rw[step, 0, FIELDS + l] = w1[l, PAD + ROWS - 2:PAD + ROWS, :]
                rw[step, 1, FIELDS + l] = w1[l, PAD:PAD + 2, :]
                return carry
            lax.fori_loop(0, LEVELS, winds_of, 0, unroll=4)
        for way in (SOUTH, NORTH):
            @pl.when(has[way])
            def _():
                rows_copy(step, way).start()

    def give_first_halo(state):
        pack_columns(0, state, 2)
        pl.semaphore_wait(barrier, expect)
        send_columns(0, 2)
        pack_columns(0, state, 3)
        send_columns(0, 3)
        loads[2].wait()
        loads[3].wait()
        give_rows(0, state)
        for group in range(2):
            pack_columns(0, state, group)
            send_columns(0, group)

    def take_rows(step, state):
        for way, came in ((SOUTH, NORTH), (NORTH, SOUTH)):
            @pl.when(has[came])
            def _():
                rows_copy(step, way).wait_recv()

        def rows_of(f, carry):
            state[f, PAD - 2:PAD, :] = rwr[step, 0, f]
            state[f, PAD + ROWS:PAD + ROWS + 2, :] = rwr[step, 1, f]
            return carry
        lax.fori_loop(0, FIELDS, rows_of, 0, unroll=8)
        if step == 0:
            def winds_of(l, carry):
                w1[l, PAD - 2:PAD, :] = rwr[step, 0, FIELDS + l]
                w1[l, PAD + ROWS:PAD + ROWS + 2, :] = rwr[step, 1, FIELDS + l]
                return carry
            lax.fori_loop(0, LEVELS, winds_of, 0, unroll=4)
    def take_columns(step, groups):
        for group in groups:
            for way, came in ((EAST, WEST), (WEST, EAST)):
                @pl.when(has[came])
                def _():
                    columns_copy(step, way, group).wait_recv()

            def unpack(g, carry):
                rows = pl.ds(pl.multiple_of(g * 8, 8), 8)
                unpacked(step, group, g, pkr[step, EAST, group, rows, :], pkr[step, WEST, group, rows, :])
                return carry
            lax.fori_loop(0, ROWS // 8, unpack, 0, unroll=2)

    def patch_copy(way):
        return pltpu.make_async_remote_copy(
            src_ref=pt, dst_ref=ptr.at[way], send_sem=psem.at[0, way], recv_sem=psem.at[1, way],
            device_id=beside[way], device_id_type=MESH)

    def patch_columns(step, state):
        for edge, g in ((0, 0), (lat_n - 1, ROWS // 8 - 1)):
            @pl.when(lat == edge)
            def _():
                for group in range(3):
                    pt[group] = packed(step, state, group, g)
        for way in (EAST, WEST):
            @pl.when(has[way])
            def _():
                patch_copy(way).start()

    def take_patch(step):
        for way in (EAST, WEST):
            @pl.when(has[way ^ 1])
            def _():
                patch_copy(way).wait_recv()
        for edge, g in ((0, 0), (lat_n - 1, ROWS // 8 - 1)):
            @pl.when(lat == edge)
            def _():
                for group in range(3):
                    unpacked(step, group, g, ptr[EAST, group], ptr[WEST, group])

    def sent_halo(step):
        for way in range(4):
            @pl.when(has[way])
            def _():
                if way in (EAST, WEST):
                    for group in range(groups_of(step)):
                        columns_copy(step, way, group).wait_send()
                    if step > 0:
                        pl.when(is_band)(patch_copy(way).wait_send)
                else:
                    rows_copy(step, way).wait_send()

    def pivots(l, carry):
        for g in range(ROWS // CHUNK):
            rows = pl.ds(g * CHUNK, CHUNK)
            low = mx[l, rows, :]
            high = mx[l + 1, rows, :]
            inv = 1.0 / (1.0 + low + high - low * rt[l, rows, :])
            iv[l, rows, :] = inv
            rt[l + 1, rows, :] = high * inv
            cf[l, 9, rows, :] = low * inv
        return carry

    def coefficients(l, carry):
        for g in range(ROWS // CHUNK):
            rows = pl.ds(g * CHUNK, CHUNK)
            w = w0[l, rows, :]
            beyond = hb[FIELDS + l, rows, :]
            w_east = pltpu.roll(jnp.where(lane_c < 1, beyond, w), COLS - 1, 1)
            w_west = pltpu.roll(jnp.where(lane_c >= COLS - 1, beyond, w), 1, 1)
            base = PAD + g * CHUNK
            v = w1[l, base:base + CHUNK, :]
            v_next = w1[l, base + 1:base + CHUNK + 1, :]
            v_prev = w1[l, base - 1:base + CHUNK - 1, :]

            def parts(face):
                face = face * (1.0 / 12.0)
                return jnp.maximum(face, 0.0), jnp.minimum(face, 0.0)

            pe, me_ = parts(w + w_east)
            pw, mw = parts(w + w_west)
            pn, mn = parts(v + v_next)
            ps, ms = parts(v + v_prev)
            inv = iv[l, rows, :]
            centre = 1.0 + (2.0 * (pw - me_) + 5.0 * (mw - pe)) + (2.0 * (ps - mn) + 5.0 * (ms - pn))
            for i, c in enumerate((
                centre,
                -pw, 5.0 * pw + 2.0 * mw + pe, -mw - 2.0 * pe - 5.0 * me_, me_,
                -ps, 5.0 * ps + 2.0 * ms + pn, -ms - 2.0 * pn - 5.0 * mn, mn,
            )):
                cf[l, i, rows, :] = c * inv
        return carry

    def forward(state, new, chunks):
        for g in chunks:
            prev[:, g * CHUNK:g * CHUNK + CHUNK, :] = jnp.zeros((2, CHUNK, COLS), jnp.float32)

        def level(l, carry):
            for g in chunks:
                rows = pl.ds(g * CHUNK, CHUNK)
                base = PAD + g * CHUNK
                for t in range(2):
                    f = t * LEVELS + l
                    q = state[f, base:base + CHUNK, :]
                    beyond = hb[f, rows, :]
                    x = cf[l, 0, rows, :] * q
                    x += cf[l, 1, rows, :] * pltpu.roll(jnp.where(lane_c >= COLS - 2, beyond, q), 2, 1)
                    x += cf[l, 2, rows, :] * pltpu.roll(jnp.where(lane_c >= COLS - 1, beyond, q), 1, 1)
                    x += cf[l, 3, rows, :] * pltpu.roll(jnp.where(lane_c < 1, beyond, q), COLS - 1, 1)
                    x += cf[l, 4, rows, :] * pltpu.roll(jnp.where(lane_c < 2, beyond, q), COLS - 2, 1)
                    x += cf[l, 5, rows, :] * state[f, base - 2:base - 2 + CHUNK, :]
                    x += cf[l, 6, rows, :] * state[f, base - 1:base - 1 + CHUNK, :]
                    x += cf[l, 7, rows, :] * state[f, base + 1:base + 1 + CHUNK, :]
                    x += cf[l, 8, rows, :] * state[f, base + 2:base + 2 + CHUNK, :]
                    x += cf[l, 9, rows, :] * prev[t, rows, :]
                    prev[t, rows, :] = x
                    new[f, base:base + CHUNK, :] = x
            return carry
        lax.fori_loop(0, LEVELS, level, 0, unroll=12 // len(chunks))

    def backward(new, chunks):
        def level(i, carry):
            l = LEVELS - 2 - i
            for g in chunks:
                rows = pl.ds(g * CHUNK, CHUNK)
                base = PAD + g * CHUNK
                for t in range(2):
                    f = t * LEVELS + l
                    x = new[f, base:base + CHUNK, :] + rt[l + 1, rows, :] * prev[t, rows, :]
                    prev[t, rows, :] = x
                    new[f, base:base + CHUNK, :] = x
            return carry
        lax.fori_loop(0, LEVELS - 1, level, 0, unroll=5)

    def to_mid(step, k):
        mlat, mlon = mid_place(k)
        return pltpu.make_async_remote_copy(
            src_ref=pay.at[step, k], dst_ref=inb[step].at[me], send_sem=p1s.at[step],
            recv_sem=p1r.at[step], device_id=(other, mlat, mlon), device_id_type=MESH)

    def to_band(step, d):
        return pltpu.make_async_remote_copy(
            src_ref=ob.at[step, pl.ds(2 * d, 2)], dst_ref=rb.at[step, mid_id],
            send_sem=p2bs.at[step], recv_sem=p2br.at[step],
            device_id=(panel, (d // lon_n) * (lat_n - 1), d % lon_n), device_id_type=MESH)

    def to_side(step, e):
        return pltpu.make_async_remote_copy(
            src_ref=ob.at[step, 4 * lon_n + e], dst_ref=rs.at[step, mid_id],
            send_sem=p2s.at[step], recv_sem=p2r.at[step],
            device_id=(panel, e % lat_n, (e // lat_n) * (lon_n - 1)), device_id_type=MESH)

    def all_of(ref, sem):
        pltpu.make_async_copy(ref, ref, sem).wait()

    def provide(step, new, tiles):
        flat = new.reshape(FIELDS * TALL, COLS)
        lane_f = lax.broadcasted_iota(jnp.int32, (FIELDS, COLS), 1)
        total = jnp.zeros((FIELDS, COLS), jnp.float32)
        for pair in range(2):
            cells = jnp.zeros((FIELDS, COLS), jnp.float32)
            for s in range(2):
                tile = tiles[2 * pair + s]
                first = PAD + (tile // 8) * 4
                for r in range(4):
                    row = flat[pl.ds(first + r, FIELDS, stride=TALL), :]
                    shift = (2 * COLS + 64 * s + 16 * r - 16 * (tile % 8)) % COLS
                    row = pltpu.roll(row, shift, 1)
                    cells = jnp.where(lane_f // 16 == 4 * s + r, row, cells)
            w = bd[128 * pair:128 * pair + 128, :]
            rest = cells
            for part in range(3):
                piece = rest.astype(jnp.bfloat16)
                total += jnp.dot(piece, w, preferred_element_type=jnp.float32)
                if part < 2:
                    rest = rest - piece.astype(jnp.float32)
        pay[step] = total.reshape(MIDS, SHARE, COLS)

    def route(step):
        def send(k, carry):
            to_mid(step, k).start()
            return carry
        lax.fori_loop(0, MIDS, send, 0)

    def sort_and_send(step):
        @pl.when(is_mid)
        def _():
            if step == 0:
                pairs = ssrc.shape[1] // 2
                shape = (pairs, 2 * pairs)
                row = jnp.where(panel == 0, vsrc[0:1, :], vsrc[1:2, :]).astype(jnp.float32)
                row = jnp.broadcast_to(row, shape)
                lane = lax.broadcasted_iota(jnp.int32, shape, 1)
                pair = lax.broadcasted_iota(jnp.int32, shape, 0)
                own = jnp.sum(jnp.where(lane == 2 * pair, row, 0.0), axis=1, keepdims=True)
                same = (row == own) & (lane % 2 == 0) & (lane < 2 * pair)
                second = jnp.max(jnp.where(same, 1.0, 0.0), axis=1, keepdims=True)
                hs[...] = jnp.broadcast_to(second, (pairs, COLS)).reshape(pairs // 8, 8, COLS)
            all_of(inb[step], p1r.at[step])
            lane_s = lax.broadcasted_iota(jnp.int32, (SHARE, COLS), 1)
            batch = 8

            def sort(i):
                done = []
                for j in range(batch):
                    u = i * batch + j
                    a = inb[step][ssrc[panel, 4 * u]]
                    b = inb[step][ssrc[panel, 4 * u + 2]]
                    line = hs[batch // 4 * i + j // 4]
                    second_a = line[2 * j % 8:2 * j % 8 + 1, :] > 0.5
                    second_b = line[2 * j % 8 + 1:2 * j % 8 + 2, :] > 0.5
                    a = jnp.where(second_a, pltpu.roll(a, 64, 1), a)
                    b = jnp.where(second_b, b, pltpu.roll(b, 64, 1))
                    done.append(jnp.where(lane_s < 64, a, b))
                for j in range(batch):
                    ob[step, i * batch + j] = done[j]

            def sides(i, carry):
                sort(4 * lon_n // batch + i)
                for j in range(batch):
                    to_side(step, batch * i + j).start()
                return carry
            lax.fori_loop(0, 2 * lat_n // batch, sides, 0)

            def bands(i, carry):
                sort(i)
                for j in range(batch // 2):
                    to_band(step, batch // 2 * i + j).start()
                return carry
            lax.fori_loop(0, 4 * lon_n // batch, bands, 0)

    def side_lines(step):
        all_of(rs.at[step], p2r.at[step])
        dense[0, 0:FIELDS, :] = rs[step].reshape(FIELDS, COLS)
        flip[...] = jnp.transpose(dense[0])
        first = flip[pl.ds(0, ROWS, stride=2), :]
        second = pltpu.roll(flip[pl.ds(1, ROWS, stride=2), :], 1, 1)
        even = lax.broadcasted_iota(jnp.int32, (ROWS, COLS), 1) % 2 == 0
        start = jnp.where(lon == 0, 0, COLS - 2)
        return (pltpu.roll(jnp.where(even, first, second), start, 1),
                pltpu.roll(jnp.where(even, second, first), start, 1))

    def band_lines(step):
        all_of(rb.at[step], p2br.at[step])
        lane_f = lax.broadcasted_iota(jnp.int32, (FIELDS, COLS), 1)
        lines = []
        for r in range(2):
            line = jnp.zeros((FIELDS, COLS), jnp.float32)
            for u in range(2):
                tiles = rb[step, :, u].reshape(FIELDS, COLS)
                for s in range(4):
                    moved = pltpu.roll(tiles, (2 * COLS + 64 * u - 16 * s - 16 * r) % COLS, 1)
                    line = jnp.where(lane_f // 16 == 4 * u + s, moved, line)
            lines.append(line)
        return lines

    def fill_column(new, g):
        start = jnp.where(lon == 0, 0, COLS - 2)
        rows = pl.ds(pl.multiple_of(PAD + g * 8, 8), 8)
        bare = pl.ds(pl.multiple_of(g * 8, 8), 8)
        pair = dense[0, bare, :], dense[1, bare, :]
        for f in range(FIELDS):
            a = pltpu.roll(pair[f % 2], COLS - f, 1) if f else pair[0]
            new[f, rows, :] = jnp.where(lane8 // 2 == start // 2, a, new[f, rows, :])

    def fill_middle(new):
        def column(g, carry):
            fill_column(new, g)
            return carry
        lax.fori_loop(1, ROWS // 8 - 1, column, 0)

    def fill(step, new):
        @pl.when(is_side)
        def _():
            dense[0, 0:ROWS, :], dense[1, 0:ROWS, :] = side_lines(step)

            def column(i, carry):
                fill_column(new, i * (ROWS // 8 - 1))
                return carry
            lax.fori_loop(0, 2, column, 0)

        @pl.when(is_band)
        def _():
            lines = band_lines(step)
            flat = new.reshape(FIELDS * TALL, COLS)
            for r in range(2):
                @pl.when(lat == 0)
                def _():
                    flat[pl.ds(PAD + r, FIELDS, stride=TALL), :] = lines[r]

                @pl.when(lat == lat_n - 1)
                def _():
                    flat[pl.ds(PAD + ROWS - 2 + r, FIELDS, stride=TALL), :] = lines[r]

    def hand_on(step):
        @pl.when(is_side)
        def _():
            sides_out[0], sides_out[1] = side_lines(step)

        @pl.when(is_band)
        def _():
            bands_out[0], bands_out[1] = band_lines(step)

    def pick_weights(strips):
        entries = wts.shape[1]
        lane = lax.broadcasted_iota(jnp.int32, (entries, COLS), 1)
        wanted = jnp.zeros((entries, COLS), jnp.int32)
        for b in range(4):
            wanted = jnp.where(lane // 32 == b, strips[b], wanted)
        entry = lax.broadcasted_iota(jnp.int32, (entries, COLS), 0)
        one_hot = jnp.where(entry == wanted, 1.0, 0.0).astype(jnp.bfloat16)
        lane_k = lax.broadcasted_iota(jnp.int32, (64, COLS), 1)

        def cell(c, total):
            rows = wts[pl.ds(pl.multiple_of(c * 64, 64), 64), :]
            mine = jnp.dot(rows, one_hot, preferred_element_type=jnp.float32)
            return jnp.where(lane_k % 32 == c, mine, total)
        total = lax.fori_loop(0, 32, cell, jnp.zeros((64, COLS), jnp.float32), unroll=4)
        for b in range(4):
            bd[64 * b:64 * b + 64, :] = jnp.where(lane_k // 32 == b, total, 0.0).astype(jnp.bfloat16)

    give_first_halo(sa)

    def look(i, found):
        first, second = found
        for j in range(8):
            m = 8 * i + j
            hit = ssrc[other, 2 * m] == me
            second = jnp.where(hit & (first >= 0), m, second)
            first = jnp.where(hit & (first < 0), m, first)
        return first, second
    found = lax.fori_loop(0, ssrc.shape[1] // 16, look, (jnp.int32(-1), jnp.int32(-1)))
    found = [jnp.maximum(m, 0) for m in found]
    strips = [2 * m + s for m in found for s in range(2)]
    tiles = [stile[other, strip] for strip in strips]

    loads[4].wait()
    lax.fori_loop(0, LEVELS, pivots, 0, unroll=2)
    loads[5].wait()
    pick_weights(strips)
    take_rows(0, sa)
    take_columns(0, (2, 3))
    lax.fori_loop(0, LEVELS, coefficients, 0, unroll=3)
    take_columns(0, (0, 1))
    for step in range(STEPS):
        state, new = (sa, sb) if step % 2 == 0 else (sb, sa)
        if step == 0:
            inner, outer = (), tuple(range(ROWS // CHUNK))
        else:
            inner, outer = tuple(range(1, ROWS // CHUNK - 1)), (0, ROWS // CHUNK - 1)
            forward(state, new, inner)
            backward(new, inner)
            pl.when(is_band)(lambda: take_patch(step))

            @pl.when(is_side)
            def _():
                take_rows(step, state)
        forward(state, new, outer)
        backward(new, outer)
        if step == STEPS - 1:
            store = pltpu.make_async_copy(new.at[:, pl.ds(PAD, ROWS), :], out_hbm, lsem.at[0])
            store.start()
        provide(step, new, tiles)
        route(step)
        if step == STEPS - 1:
            sort_and_send(step)
            hand_on(step)
        else:
            later = step + 1
            for group in range(3):
                pack_columns(later, new, group)
                send_columns(later, group)
            pl.when(jnp.logical_not(is_side))(lambda: give_rows(later, new))
            sort_and_send(step)
            take_columns(later, (0, 1, 2))
            pl.when(jnp.logical_not(is_side))(lambda: take_rows(later, new))
            fill(step, new)

            @pl.when(is_side)
            def _():
                give_rows(later, new)
            pl.when(is_band)(lambda: patch_columns(later, new))
            pl.when(is_side)(lambda: fill_middle(new))

    for step in range(STEPS):
        sent_halo(step)
        all_of(pay.at[step], p1s.at[step])

        @pl.when(is_mid)
        def _():
            all_of(ob.at[step, pl.ds(0, 4 * lon_n)], p2bs.at[step])
            all_of(ob.at[step, pl.ds(4 * lon_n, 2 * lat_n)], p2s.at[step])
    store.wait()


def last_fill(lat_n, lon_n, chunks, state, sides, bands, out, held, side, band, rsem, wsem, lsem):
    lat = lax.axis_index("lat")
    lon = lax.axis_index("lon")
    count = FIELDS // chunks
    is_side = (lon == 0) | (lon == lon_n - 1)
    is_band = (lat == 0) | (lat == lat_n - 1)
    start = jnp.where(lon == 0, 0, COLS - 2)
    lane = lax.broadcasted_iota(jnp.int32, (ROWS, COLS), 1)
    get_side = pltpu.make_async_copy(sides, side, lsem.at[0])
    get_band = pltpu.make_async_copy(bands, band, lsem.at[1])
    pl.when(is_side)(get_side.start)
    pl.when(is_band)(get_band.start)
    parts = [pl.ds(c * count, count) for c in range(chunks)]
    reads = [pltpu.make_async_copy(state.at[p], held.at[p], rsem.at[c]) for c, p in enumerate(parts)]
    writes = [pltpu.make_async_copy(held.at[p], out.at[p], wsem.at[c]) for c, p in enumerate(parts)]
    for read in reads:
        read.start()
    pl.when(is_side)(get_side.wait)
    pl.when(is_band)(get_band.wait)
    for c in range(chunks):
        reads[c].wait()
        fields = range(c * count, c * count + count)

        @pl.when(is_side)
        def _():
            for f in fields:
                a = pltpu.roll(side[f % 2], COLS - f, 1) if f else side[0]
                held[f] = jnp.where(lane // 2 == start // 2, a, held[f])

        for edge, row in ((0, 0), (lat_n - 1, ROWS - 2)):
            @pl.when(lat == edge)
            def _():
                for f in fields:
                    for r in range(2):
                        held[f, row + r:row + r + 1, :] = band[r, f:f + 1, :]

        writes[c].start()
    for write in writes:
        write.wait()


def on_device(lat_n, lon_n, tracers, winds, mixing, strip_source, strip_tile, weights):
    f32 = jnp.float32
    vm = pltpu.VMEM
    dma = pltpu.SemaphoreType.DMA
    devices = lat_n * lon_n
    tiles_out = 4 * lon_n + 2 * lat_n
    anywhere = pl.BlockSpec(memory_space=pl.ANY)
    smem = pl.BlockSpec(memory_space=pltpu.SMEM)
    in_vmem = pl.BlockSpec(memory_space=pltpu.VMEM)
    state, sides, bands = pl.pallas_call(
        functools.partial(kernel, lat_n, lon_n),
        out_shape=(
            jax.ShapeDtypeStruct((FIELDS, ROWS, COLS), f32),
            jax.ShapeDtypeStruct((2, ROWS, COLS), f32),
            jax.ShapeDtypeStruct((2, FIELDS, COLS), f32),
        ),
        in_specs=[smem, smem, in_vmem, anywhere, anywhere, anywhere, anywhere],
        out_specs=(anywhere, in_vmem, in_vmem),
        scratch_shapes=[
            vm((FIELDS, TALL, COLS), f32),
            vm((FIELDS, TALL, COLS), f32),
            vm((LEVELS, ROWS, COLS), f32),
            vm((LEVELS, TALL, COLS), f32),
            vm((LEVELS + 1, ROWS, COLS), f32),
            vm((LEVELS, 10, ROWS, COLS), f32),
            vm((LEVELS + 1, ROWS, COLS), f32),
            vm((LEVELS, ROWS, COLS), f32),
            vm((32 * 64, weights.shape[1]), weights.dtype),
            vm((256, COLS), jnp.bfloat16),
            vm((STEPS, 4, ROWS, COLS), f32),
            vm((STEPS, 2, 4, ROWS, COLS), f32),
            vm((3, 8, COLS), f32),
            vm((2, 3, 8, COLS), f32),
            vm((FIELDS + LEVELS, ROWS, COLS), f32),
            vm((STEPS, 2, FIELDS + LEVELS, 2, COLS), f32),
            vm((STEPS, 2, FIELDS + LEVELS, 2, COLS), f32),
            vm((2, ROWS, COLS), f32),
            vm((STEPS, MIDS, SHARE, COLS), f32),
            vm((devices, SHARE, COLS), f32),
            vm((devices, SHARE, COLS), f32),
            vm((strip_source.shape[1] // 16, 8, COLS), f32),
            vm((STEPS, tiles_out, SHARE, COLS), f32),
            vm((STEPS, MIDS, 2, SHARE, COLS), f32),
            vm((STEPS, MIDS, SHARE, COLS), f32),
            vm((2, 128, COLS), f32),
            vm((128, COLS), f32),
            dma((6,)),
            dma((STEPS, 4, 4)),
            dma((STEPS, 4, 4)),
            dma((2, 2)),
            dma((STEPS,)),
            dma((STEPS,)),
            dma((STEPS,)),
            dma((STEPS,)),
            dma((STEPS,)),
            dma((STEPS,)),
        ],
        compiler_params=pltpu.CompilerParams(
            collective_id=0, has_side_effects=True, vmem_limit_bytes=56 * 1024 * 1024),
    )(
        strip_source, strip_tile, strip_source,
        tracers.reshape(FIELDS, ROWS, COLS),
        winds.reshape(2, LEVELS, ROWS, COLS),
        mixing.reshape(LEVELS - 1, ROWS, COLS),
        jnp.transpose(weights, (0, 2, 3, 1)).reshape(2, 32 * 64, weights.shape[1]),
    )
    chunks = 4
    out = pl.pallas_call(
        functools.partial(last_fill, lat_n, lon_n, chunks),
        out_shape=jax.ShapeDtypeStruct((FIELDS, ROWS, COLS), f32),
        in_specs=[anywhere, anywhere, anywhere],
        out_specs=anywhere,
        scratch_shapes=[
            vm((FIELDS, ROWS, COLS), f32),
            vm((2, ROWS, COLS), f32),
            vm((2, FIELDS, COLS), f32),
            dma((chunks,)),
            dma((chunks,)),
            dma((2,)),
        ],
        compiler_params=pltpu.CompilerParams(vmem_limit_bytes=56 * 1024 * 1024),
    )(state, sides, bands)
    return out.reshape(tracers.shape)


def solution(mesh):
    return jax.shard_map(
        functools.partial(on_device, mesh.shape["lat"], mesh.shape["lon"]),
        mesh=mesh,
        in_specs=(
            P("panel", None, None, "lat", "lon"),
            P("panel", None, None, "lat", "lon"),
            P("panel", None, "lat", "lon"),
            P(),
            P(),
            P(),
        ),
        out_specs=P("panel", None, None, "lat", "lon"),
        check_vma=False,
    )
```
